128 devices in a mesh: lat: 8 (over y, x_hi), lon: 16 (over x_lo, z, core).
Axes of the slice: x: 4 (x_hi: 2, x_lo: 2; x = x_hi * 2 + x_lo), y: 4, z: 4, core: 2. Of those that a mesh axis runs over, the one named last changes fastest.
Arguments:
- patches: bfloat16 [128, 512, 4, 512], P('lat', 'lon'), may hold values from -6 to 6
- qkv_weight: bfloat16 [2, 512, 1536], replicated, may hold values from -1 to 1
- proj_weight: bfloat16 [2, 512, 512], replicated, may hold values from -0.25 to 0.25
- up_weight: bfloat16 [2, 512, 2048], replicated, may hold values from -0.25 to 0.25
- down_weight: bfloat16 [2, 2048, 512], replicated, may hold values from -0.125 to 0.125
- merge_weight: bfloat16 [2048, 1024], replicated, may hold values from -0.125 to 0.125
Outputs:
- merged: bfloat16 [64, 256, 4, 1024], P('lat', 'lon')
The draws below stay inside these ranges and needn't reach their ends.
All inputs are finite; a program needn't handle non-finite values.
Results may differ from the reference program's by a relative error of at most 0.015.
Values may be sent and summed in bfloat16 or wider, within the bound.
No kernel may reach another device: no remote copies, remote signals or barrier semaphores. Data moves between devices by JAX's collectives and lax.ppermute only.
A program may use at most 192 MiB of HBM per device.

```python
import jax
import jax.numpy as jnp
from jax import lax

C = 512
HEADS = 8
FF = 2048
LEVELS = 4
NH = 128
NW = 512


def draw_qkv_weight(key, part):
    key = jax.random.fold_in(key, 7)
    key_one = jax.random.fold_in(key, 0)
    initial = jax.random.truncated_normal(key_one, -6.0, 6.0, (2, C, 3 * C), jnp.float32) * C ** (-0.5)
    return jnp.clip(initial, -1.0, 1.0).astype(jnp.bfloat16)


def block_scale(stream_key, extent, cuts, least, top_value):
    level = 1.0
    for axis_at, blocks in cuts:
        draws = jax.random.uniform(jax.random.fold_in(jax.random.fold_in(stream_key, 6), axis_at), (blocks,), jnp.float32, least / len(cuts), top_value / len(cuts))
        level = level * jnp.repeat(jnp.exp(draws), extent[axis_at] // blocks).reshape((-1,) + (1,) * (len(extent) - 1 - axis_at))
    return level


def scatter_about(key, shape, deviation, most, pieces=(), kind=jnp.bfloat16):
    drawn = deviation * jax.random.normal(key, shape, jnp.float32)
    if pieces:
        drawn = drawn * block_scale(key, shape, pieces, -0.22, 0.18)
    return jnp.clip(drawn, -most, most).astype(kind)


def setup_inputs(seed: int = 0) -> dict:
    key_list = jax.random.split(jax.random.key(seed), 7)
    patches = scatter_about(key_list[0], (NH, NW, LEVELS, C), 1.0, 6.0, ((0, 8), (1, 16)))
    qkv_weight = draw_qkv_weight(jax.random.fold_in(key_list[6], 71), 0)
    proj_weight = scatter_about(key_list[2], (2, C, C), C ** -0.5, 0.25)
    up_weight = scatter_about(key_list[3], (2, C, FF), C ** -0.5, 0.25)
    down_weight = scatter_about(key_list[4], (2, FF, C), FF ** -0.5, 0.125)
    merge_weight = scatter_about(key_list[5], (4 * C, 2 * C), (4 * C) ** -0.5, 0.125)
    return dict(patches=patches, qkv_weight=qkv_weight, proj_weight=proj_weight, up_weight=up_weight, down_weight=down_weight, merge_weight=merge_weight)


def normalize(values):
    centre = lax.optimization_barrier(jnp.mean(values, axis=-1, keepdims=True))
    spread = lax.optimization_barrier(jnp.mean((values - centre) ** 2, axis=-1, keepdims=True))
    return (values - centre) * lax.rsqrt(spread + 1e-05)

def partition(grid):
    rows, cols, levels, width = grid.shape
    grid = grid.reshape(rows // 8, 8, cols // 8, 8, levels, width).transpose(0, 2, 1, 3, 4, 5)
    return grid.reshape(rows // 8, cols // 8, 64 * levels, width)

def unpartition(windows, rows, cols):
    wrows, wcols, count, width = windows.shape
    levels = count // 64
    grid = windows.reshape(wrows, wcols, 8, 8, levels, width).transpose(0, 2, 1, 3, 4, 5)
    return grid.reshape(rows, cols, levels, width)

def attend(queries, key_rows, value_rows, key_ok, group):
    count, tokens, width = queries.shape
    depth = width // HEADS
    query_heads = queries.astype(jnp.float32).reshape(count, tokens, HEADS, depth)
    key_heads = key_rows.astype(jnp.float32).reshape(count, tokens, HEADS, depth)
    value_heads = value_rows.astype(jnp.float32).reshape(count, tokens, HEADS, depth)
    scores = jnp.einsum('nqhd,nkhd->nhqk', query_heads, key_heads) * depth ** (-0.5)
    allowed = key_ok[:, None, None, :] & (group[:, None] == group[None, :])[None, None]
    scores = jnp.where(allowed, scores, -1e+30)
    highest = lax.optimization_barrier(jnp.max(scores, axis=-1, keepdims=True))
    probs = jnp.exp(scores - highest)
    probs = (probs / lax.optimization_barrier(jnp.sum(probs, axis=-1, keepdims=True))).astype(jnp.bfloat16)
    output = jnp.einsum('nhqk,nkhd->nqhd', probs.astype(jnp.float32), value_heads)
    return output.reshape(count, tokens, width).astype(jnp.bfloat16)

def section_block(stream, qkv_weight, proj_weight, up_weight, down_weight, shifted):
    rows, cols, levels, width = stream.shape
    normed = normalize(stream).astype(jnp.bfloat16)
    projected = jnp.dot(normed.reshape(-1, width), qkv_weight, preferred_element_type=jnp.float32)
    projected = projected.astype(jnp.bfloat16).reshape(rows, cols, levels, 3 * width)
    if shifted:
        projected = jnp.roll(projected, 4, axis=1)
        projected = jnp.pad(projected, ((4, 4), (0, 0), (0, 0), (0, 0)))
        positions = jnp.arange(rows + 8)
        row_ok = (positions >= 4) & (positions < rows + 4)
        offset = 1
    else:
        row_ok = jnp.ones((rows,), dtype=bool)
        offset = 0
    windows = partition(projected)
    tokens = windows.shape[2]
    key_ok = row_ok.reshape(-1, 8)[:, jnp.arange(tokens) // (8 * levels)]
    group = (jnp.arange(tokens) % levels + offset) // 2

    def one_row(item):
        window_row, row_keys = item
        spread_ok = jnp.broadcast_to(row_keys[None, :], (window_row.shape[0], tokens))
        return attend(window_row[..., :width], window_row[..., width:2 * width], window_row[..., 2 * width:], spread_ok, group)
    mixed = lax.map(one_row, (windows, key_ok))
    mixed = unpartition(mixed, projected.shape[0], cols)
    if shifted:
        mixed = jnp.roll(mixed[4:-4], -4, axis=1)
    update = jnp.dot(mixed.reshape(-1, width), proj_weight, preferred_element_type=jnp.float32)
    stream = stream + update.reshape(stream.shape)
    normed = normalize(stream).astype(jnp.bfloat16)
    hidden = jax.nn.gelu(jnp.dot(normed.reshape(-1, width), up_weight, preferred_element_type=jnp.float32), approximate=True).astype(jnp.bfloat16)
    update = jnp.dot(hidden, down_weight, preferred_element_type=jnp.float32)
    return stream + update.reshape(stream.shape)

def reference(patches, qkv_weight, proj_weight, up_weight, down_weight, merge_weight):
    stream = patches.astype(jnp.float32)
    stream = section_block(stream, qkv_weight[0], proj_weight[0], up_weight[0], down_weight[0], False)
    stream = stream.astype(jnp.bfloat16).astype(jnp.float32)
    stream = section_block(stream, qkv_weight[1], proj_weight[1], up_weight[1], down_weight[1], True)
    gathered = jnp.concatenate([stream[0::2, 0::2], stream[1::2, 0::2], stream[0::2, 1::2], stream[1::2, 1::2]], axis=-1)
    normed = normalize(gathered).astype(jnp.bfloat16)
    rows, cols, levels, width = normed.shape
    merged = jnp.dot(normed.reshape(-1, width), merge_weight, preferred_element_type=jnp.float32)
    return merged.reshape(rows, cols, levels, -1).astype(jnp.bfloat16)
```

```python
import functools

import jax
import jax.numpy as jnp
from jax import lax
from jax.experimental import pallas as pl
from jax.experimental.pallas import tpu as pltpu
from jax.sharding import PartitionSpec as P
import numpy as np

HEADS = 8
PLAIN = ((0, 2), (2, 4))
SHIFTED = ((0, 1), (1, 3), (3, 4))
VMEM_LIMIT = 56 * 1024 * 1024


def token_order():
    order = []
    for quarter_row in range(2):
        for quarter_col in range(2):
            for level in range(4):
                for r2 in range(2):
                    for c2 in range(2):
                        for q in range(4):
                            r = quarter_row * 4 + r2 * 2 + q % 2
                            c = quarter_col * 4 + c2 * 2 + q // 2
                            order.append((r * 8 + c) * 4 + level)
    return np.array(order)


def merged_order():
    order = []
    for r in range(4):
        for c in range(4):
            for level in range(4):
                order.append(((r // 2 * 2 + c // 2) * 4 + level) * 4 + (r % 2) * 2 + c % 2)
    return np.array(order)


def one_hot(order):
    return jnp.asarray(order[:, None] == np.arange(order.size)[None, :], jnp.bfloat16)


def normalize(values):
    centre = jnp.mean(values, axis=-1, keepdims=True)
    values = values - centre
    spread = jnp.mean(values * values, axis=-1, keepdims=True)
    return values * lax.rsqrt(spread + 1e-05)


def dot(a, b):
    return jnp.dot(a, b, preferred_element_type=jnp.float32)


def take_levels(values, low, high):
    return jnp.concatenate([values[t * 64 + low * 16 : t * 64 + high * 16] for t in range(4)], axis=0)


def attend(qkv, groups, cut):
    outs = []
    for low, high in groups:
        rows = take_levels(qkv, low, high)
        tokens = rows.shape[0]
        lane = lax.broadcasted_iota(jnp.int32, (tokens, 128), 1)
        even = jnp.where(lane < 64, 1.0, 0.0).astype(jnp.bfloat16)
        odd = jnp.where(lane < 64, 0.0, 1.0).astype(jnp.bfloat16)
        pairs = []
        for p in range(4):
            q = rows[:, p * 128 : (p + 1) * 128]
            k = rows[:, 512 + p * 128 : 512 + (p + 1) * 128]
            v = rows[:, 1024 + p * 128 : 1024 + (p + 1) * 128]
            keys = jnp.concatenate([k * even, k * odd], axis=0)
            values = jnp.concatenate(
                [
                    jnp.concatenate([v * even, v * odd], axis=0),
                    jnp.concatenate([even, odd], axis=0),
                ],
                axis=1,
            )
            scores = lax.dot_general(
                q, keys, (((1,), (1,)), ((), ())), preferred_element_type=jnp.float32
            )
            halves = []
            for h in range(2):
                s = scores[:, h * tokens : (h + 1) * tokens]
                if cut is not None:
                    half = tokens // 2
                    row_half = lax.broadcasted_iota(jnp.int32, s.shape, 0) >= half
                    col_half = lax.broadcasted_iota(jnp.int32, s.shape, 1) >= half
                    s = jnp.where((row_half != col_half) & cut, -1e30, s)
                highest = jnp.max(s, axis=-1, keepdims=True)
                halves.append(jnp.exp((s - highest) * 0.125).astype(jnp.bfloat16))
            probs = jnp.concatenate(halves, axis=1)
            out = dot(probs, values)
            pairs.append((out[:, :128] / out[:, 128:]).astype(jnp.bfloat16))
        outs.append((low, high, jnp.concatenate(pairs, axis=1)))
    pieces = []
    for t in range(4):
        for low, high, out in outs:
            n = (high - low) * 16
            pieces.append(out[t * n : (t + 1) * n])
    return jnp.concatenate(pieces, axis=0)


def block(stream, wqkv, wproj, wup, wdown, groups, cut):
    qkv = dot(normalize(stream).astype(jnp.bfloat16), wqkv[0]).astype(jnp.bfloat16)
    mixed = attend(qkv, groups, cut)
    stream = stream + dot(mixed, wproj[0])
    hidden = dot(normalize(stream).astype(jnp.bfloat16), wup[0])
    hidden = jax.nn.gelu(hidden, approximate=True).astype(jnp.bfloat16)
    return stream + dot(hidden, wdown[0])


def plain_kernel(x_ref, perm_ref, wqkv, wproj, wup, wdown, out_ref):
    tokens = x_ref[...].astype(jnp.float32).reshape(256, 512).astype(jnp.bfloat16)
    stream = dot(perm_ref[...], tokens)
    stream = block(stream, wqkv, wproj, wup, wdown, PLAIN, None)
    out_ref[...] = stream.astype(jnp.bfloat16).reshape(2, 2, 64, 512)


def shifted_kernel(last_ref, x_ref, perm_ref, wqkv, wproj, wup, wdown, wmerge, out_ref, scratch):
    stream = x_ref[...].reshape(256, 512).astype(jnp.float32)
    cut = (last_ref[0] == 1) & (pl.program_id(0) == 1)
    stream = block(stream, wqkv, wproj, wup, wdown, SHIFTED, cut)
    for t in range(4):
        scratch[t] = stream[:, t * 128 : (t + 1) * 128]
    pieces = [
        jnp.concatenate([scratch[t, pl.ds(q, 64, stride=4), :] for t in range(4)], axis=1)
        for q in range(4)
    ]
    gathered = jnp.concatenate(pieces, axis=1)
    normed = normalize(gathered).astype(jnp.bfloat16)
    merged = dot(normed, wmerge[...]).astype(jnp.bfloat16)
    merged = dot(perm_ref[...], merged)
    out_ref[...] = merged.reshape(4, 4, 4, 1024).astype(jnp.bfloat16)


def weight_spec(index, rows, cols):
    return pl.BlockSpec((1, rows, cols), lambda i, j: (index, 0, 0), pipeline_mode=pl.Buffered(1))


def whole_spec(shape):
    return pl.BlockSpec(shape, lambda i, j: (0,) * len(shape), pipeline_mode=pl.Buffered(1))


def weight_specs(index):
    return [
        weight_spec(index, 512, 1536),
        weight_spec(index, 512, 512),
        weight_spec(index, 512, 2048),
        weight_spec(index, 2048, 512),
    ]


def plain_block(patches, wqkv, wproj, wup, wdown):
    return pl.pallas_call(
        plain_kernel,
        grid=(2, 4),
        in_specs=[pl.BlockSpec((8, 8, 4, 512), lambda i, j: (i, j, 0, 0)), whole_spec((256, 256))]
        + weight_specs(0),
        out_specs=pl.BlockSpec((2, 2, 64, 512), lambda i, j: (i, j, 0, 0)),
        out_shape=jax.ShapeDtypeStruct((4, 8, 64, 512), jnp.bfloat16),
        compiler_params=pltpu.CompilerParams(vmem_limit_bytes=VMEM_LIMIT),
        name="plain_block",
    )(patches, one_hot(token_order()), wqkv, wproj, wup, wdown)


def shifted_block(last, quarters, wqkv, wproj, wup, wdown, wmerge):
    return pl.pallas_call(
        shifted_kernel,
        grid=(2, 4),
        in_specs=[
            pl.BlockSpec(memory_space=pltpu.SMEM),
            pl.BlockSpec((2, 2, 64, 512), lambda i, j: (i, j, 0, 0)),
            whole_spec((64, 64)),
        ]
        + weight_specs(1)
        + [whole_spec((2048, 1024))],
        out_specs=pl.BlockSpec((4, 4, 4, 1024), lambda i, j: (i, j, 0, 0)),
        out_shape=jax.ShapeDtypeStruct((8, 16, 4, 1024), jnp.bfloat16),
        scratch_shapes=[pltpu.VMEM((4, 256, 128), jnp.float32)],
        compiler_params=pltpu.CompilerParams(vmem_limit_bytes=VMEM_LIMIT),
        name="shifted_block",
    )(last, quarters, one_hot(merged_order()), wqkv, wproj, wup, wdown, wmerge)


def back(values, axis):
    count = lax.axis_size(axis)
    return lax.ppermute(values, axis, [((i + 1) % count, i) for i in range(count)])


def forth(values, axis):
    count = lax.axis_size(axis)
    return lax.ppermute(values, axis, [(i, (i + 1) % count) for i in range(count)])


def body(patches, qkv_weight, proj_weight, up_weight, down_weight, merge_weight):
    quarters = plain_block(patches, qkv_weight, proj_weight, up_weight, down_weight)
    quarters = jnp.concatenate([quarters[1:], back(quarters[:1], "lat")], axis=0)
    quarters = jnp.concatenate([quarters[:, 1:], back(quarters[:, :1], "lon")], axis=1)
    last = (lax.axis_index("lat") == lax.axis_size("lat") - 1).astype(jnp.int32).reshape(1)
    merged = shifted_block(
        last, quarters, qkv_weight, proj_weight, up_weight, down_weight, merge_weight
    )
    merged = jnp.concatenate([forth(merged[:, 14:], "lon"), merged[:, :14]], axis=1)
    return jnp.concatenate([forth(merged[6:], "lat"), merged[:6]], axis=0)


def solution(mesh):
    return jax.shard_map(
        body,
        mesh=mesh,
        in_specs=(P("lat", "lon", None, None), P(), P(), P(), P(), P()),
        out_specs=P("lat", "lon", None, None),
        check_vma=False,
    )
```

```python
import functools

import jax
import jax.numpy as jnp
from jax import lax
from jax.experimental import pallas as pl
from jax.experimental.pallas import tpu as pltpu
from jax.sharding import PartitionSpec as P
import numpy as np

HEADS = 8
PLAIN = ((0, 1), (2, 3))
SHIFTED = ((1, 2), (0, 3))
FFCHUNK = 2048
GROUP = 4
WEIGHTS = ((512, 1536), (512, 512), (512, 2048), (2048, 512))
VMEM_LIMIT = 56 * 1024 * 1024


def token_order():
    order = []
    for quarter_row in range(2):
        for quarter_col in range(2):
            for level in range(4):
                for r2 in range(2):
                    for c2 in range(2):
                        for q in range(4):
                            r = quarter_row * 4 + r2 * 2 + q % 2
                            c = quarter_col * 4 + c2 * 2 + q // 2
                            order.append((r * 8 + c) * 4 + level)
    return np.array(order)


def merged_order():
    order = []
    for r in range(4):
        for c in range(4):
            for level in range(4):
                order.append(((r // 2 * 2 + c // 2) * 4 + level) * 4 + (r % 2) * 2 + c % 2)
    return np.array(order)


def one_hot(order):
    return jnp.asarray(order[:, None] == np.arange(order.size)[None, :], jnp.bfloat16)


def normalize(values):
    centre = jnp.mean(values, axis=-1, keepdims=True)
    values = values - centre
    spread = jnp.mean(values * values, axis=-1, keepdims=True)
    return values * lax.rsqrt(spread + 1e-05)


def dot(a, b):
    return jnp.dot(a, b, preferred_element_type=jnp.float32)


def take_levels(values, levels):
    return jnp.concatenate(
        [values[t * 64 + lv * 16 : t * 64 + (lv + 1) * 16] for t in range(4) for lv in levels], axis=0
    )


def group_biases(cut):
    row = lax.broadcasted_iota(jnp.int32, (128, 128), 0)
    col = lax.broadcasted_iota(jnp.int32, (128, 128), 1)
    apart = (row // 16 % 2) != (col // 16 % 2)
    if cut is None:
        return None, jnp.where(apart, -1e30, 0.0)
    across = ((row // 64) != (col // 64)) & cut
    return jnp.where(across, -1e30, 0.0), jnp.where(across | apart, -1e30, 0.0)


def attend(qkv, groups, biases):
    outs = {}
    lane = lax.broadcasted_iota(jnp.int32, (128, 128), 1)
    even = jnp.where(lane < 64, 1.0, 0.0).astype(jnp.bfloat16)
    odd = jnp.where(lane < 64, 0.0, 1.0).astype(jnp.bfloat16)
    ones = jnp.concatenate([even, odd], axis=0)
    for levels, bias in zip(groups, biases):
        rows = take_levels(qkv, levels)
        pairs = []
        for p in range(4):
            q = rows[:, p * 128 : (p + 1) * 128]
            k = rows[:, 512 + p * 128 : 512 + (p + 1) * 128]
            v = rows[:, 1024 + p * 128 : 1024 + (p + 1) * 128]
            keys = jnp.concatenate([k * even, k * odd], axis=0)
            values = jnp.concatenate([v * even, v * odd], axis=0)
            values = jnp.concatenate([values, ones], axis=1)
            scores = lax.dot_general(
                q, keys, (((1,), (1,)), ((), ())), preferred_element_type=jnp.float32
            )
            halves = []
            for h in range(2):
                s = scores[:, h * 128 : (h + 1) * 128]
                if bias is not None:
                    s = s + bias
                highest = jnp.max(s, axis=-1, keepdims=True)
                halves.append(jnp.exp((s - highest) * 0.125).astype(jnp.bfloat16))
            out = dot(jnp.concatenate(halves, axis=1), values)
            pairs.append((out[:, :128] * (1.0 / out[:, 128:])).astype(jnp.bfloat16))
        out = jnp.concatenate(pairs, axis=1)
        for t in range(4):
            for n, lv in enumerate(levels):
                at = (t * len(levels) + n) * 16
                outs[t, lv] = out[at : at + 16]
    return jnp.concatenate([outs[t, lv] for t in range(4) for lv in range(4)], axis=0)


def gelu(x):
    half = 0.5 * x
    return half + half * jnp.tanh(x * (0.7978845608028654 + 0.035677408136300125 * (x * x)))


def block(streams, weights, groups, biases):
    normed = [normalize(s).astype(jnp.bfloat16) for s in streams]
    wqkv = weights[0]()
    qkvs = [dot(n, wqkv[...]).astype(jnp.bfloat16) for n in normed]
    mixed = [attend(q, groups, biases) for q in qkvs]
    wproj = weights[1]()
    streams = [s + dot(m, wproj[...]) for s, m in zip(streams, mixed)]
    normed = [normalize(s).astype(jnp.bfloat16) for s in streams]
    hidden = [[] for _ in streams]
    wup = weights[2]()
    for c in range(0, 2048, FFCHUNK):
        for n, h in zip(normed, hidden):
            h.append(gelu(dot(n, wup[:, c : c + FFCHUNK])).astype(jnp.bfloat16))
    wdown = weights[3]()
    return [s + dot(jnp.concatenate(h, axis=1), wdown[...]) for s, h in zip(streams, hidden)]


class Copies:
    def __init__(self, sems):
        self.sems, self.open = sems, []

    def start(self, source, target):
        copy = pltpu.make_async_copy(source, target, self.sems.at[len(self.open)])
        copy.start()
        self.open.append(copy)

    def wait(self, index):
        if self.open[index] is not None:
            self.open[index].wait()
            self.open[index] = None

    def later(self, source, target):
        index = len(self.open)
        self.start(source, target)

        def ready():
            self.wait(index)
            return target

        return ready

    def finish(self):
        for index in range(len(self.open)):
            self.wait(index)


def plain_kernel(row, x_hbm, perm_hbm, wqkv, wproj, wup, wdown, *rest):
    if row == 0:
        up, corner, left, inner, x, perm, b0, b1, b2, b3, done, sems = rest
    else:
        left, inner, low, x, perm, b0, b1, b2, b3, done, sems = rest
    copies = Copies(sems)
    tokens = [
        copies.later(x_hbm.at[pl.ds(row * 8, 8), pl.ds(w * 8, 8)], x.at[w]) for w in range(2)
    ]
    order = copies.later(perm_hbm, perm)
    weights = [copies.later(wqkv.at[0], b0)]
    tokens += [
        copies.later(x_hbm.at[pl.ds(row * 8, 8), pl.ds(w * 8, 8)], x.at[w]) for w in range(2, 4)
    ]
    weights += [copies.later(s.at[0], d) for s, d in ((wproj, b1), (wup, b2), (wdown, b3))]
    for g in range(0, 4, GROUP):
        streams = []
        for w in range(g, g + GROUP):
            t = tokens[w]()[...].astype(jnp.float32).reshape(256, 512).astype(jnp.bfloat16)
            streams.append(dot(order()[...], t))
        streams = block(streams, weights, PLAIN, (None, None))
        for w in range(g, g + GROUP):
            done[w] = streams[w - g].astype(jnp.bfloat16).reshape(4, 64, 512)
            for quarter in range(4):
                qr, qc = quarter // 2, 2 * w + quarter % 2
                source = done.at[w, pl.ds(quarter, 1)]
                if row == 0 and qr == 0:
                    copies.start(source, corner if qc == 0 else up.at[pl.ds(qc - 1, 1)])
                elif qc == 0:
                    copies.start(source, left.at[pl.ds(qr if row else 0, 1)])
                elif row == 0 or qr == 0:
                    copies.start(source, inner.at[pl.ds(qc - 1, 1)])
                else:
                    copies.start(source, low.at[pl.ds(qc - 1, 1)])
    copies.finish()


def merge(streams, perm, wmerge, scratch):
    for w, stream in enumerate(streams):
        for t in range(4):
            scratch[w, t] = stream[:, t * 128 : (t + 1) * 128]
    normed = []
    for w in range(len(streams)):
        pieces = [
            jnp.concatenate([scratch[w, t, pl.ds(q, 64, stride=4), :] for t in range(4)], axis=1)
            for q in range(4)
        ]
        normed.append(normalize(jnp.concatenate(pieces, axis=1)).astype(jnp.bfloat16))
    merged = dot(jnp.concatenate(normed, axis=0), wmerge()[...]).astype(jnp.bfloat16)
    return [dot(perm()[...], merged[w * 64 : (w + 1) * 64]) for w in range(len(streams))]


def shifted_kernel(count, gather, scatter, n_in, n_out, aliased, *refs):
    ins, refs = refs[:n_in], refs[n_in:]
    perm_hbm, wqkv, wproj, wup, wdown, wmerge = refs[:6]
    refs = refs[6 + aliased :]
    outs, refs = refs[:n_out], refs[n_out:]
    x, perm, b0, b1, b2, b3, b4, done, scratch, sems = refs
    copies = Copies(sems)
    tokens = []
    for w in range(count):
        tokens.append(
            [
                copies.later(ins[n].at[pl.ds(at, size)], x.at[w, pl.ds(to, size)])
                for n, at, to, size in gather[w]
            ]
        )
        if w == min(count, GROUP) - 1:
            weights = [copies.later(wqkv.at[1], b0)]
    weights += [copies.later(s.at[1], d) for s, d in ((wproj, b1), (wup, b2), (wdown, b3))]
    order = copies.later(perm_hbm, perm)
    last = copies.later(wmerge, b4)
    if count == 4:
        cut = lax.axis_index("lat") == lax.axis_size("lat") - 1
    else:
        cut = None
    biases = group_biases(cut)
    step = min(GROUP, count)
    for g in range(0, count, step):
        streams = []
        for w in range(g, g + step):
            for piece in tokens[w]:
                piece()
            streams.append(x[w].reshape(256, 512).astype(jnp.float32))
        streams = block(streams, weights, SHIFTED, biases)
        rows = merge(streams, order, last, scratch.at[pl.ds(g, step)])
        for w in range(g, g + step):
            done[w] = rows[w - g].reshape(4, 4, 4, 1024).astype(jnp.bfloat16)
            for n, r, c, to_r, to_c, size_r, size_c in scatter[w]:
                copies.start(
                    done.at[w, pl.ds(r, size_r), pl.ds(c, size_c)],
                    outs[n].at[pl.ds(to_r, size_r), pl.ds(to_c, size_c)],
                )
    copies.finish()


def finish_kernel(lat, diag, lon_low, lon, partial, out, sems):
    copies = Copies(sems)
    copies.start(lat, out.at[pl.ds(0, 2), pl.ds(2, 14)])
    copies.start(diag, out.at[pl.ds(0, 2), pl.ds(0, 2)])
    copies.start(lon, out.at[pl.ds(2, 4), pl.ds(0, 2)])
    copies.start(lon_low, out.at[pl.ds(6, 2), pl.ds(0, 2)])
    copies.finish()


ANY = pl.BlockSpec(memory_space=pl.ANY)


def quarters(count):
    return jax.ShapeDtypeStruct((count, 64, 512), jnp.bfloat16)


def merged_shape(rows, cols):
    return jax.ShapeDtypeStruct((rows, cols, 4, 1024), jnp.bfloat16)


def weight_buffers():
    return [pltpu.VMEM(shape, jnp.bfloat16) for shape in WEIGHTS]


def cost(windows, merging):
    flops = windows * (2 * 256 * (512 * 6144) + 4 * 8 * 256 * 128 * 64)
    flops += windows * merging * 2 * 64 * 2048 * 1024
    return pl.CostEstimate(flops=flops, bytes_accessed=8 << 20, transcendentals=windows * 256 * 3072)


def plain_block(row, patches, weights):
    if row == 0:
        shapes = [quarters(7), quarters(1), quarters(1), quarters(7)]
    else:
        shapes = [quarters(2), quarters(7), quarters(7)]
    return pl.pallas_call(
        functools.partial(plain_kernel, row),
        in_specs=[ANY] * 6,
        out_specs=[ANY] * len(shapes),
        out_shape=shapes,
        scratch_shapes=[
            pltpu.VMEM((4, 8, 8, 4, 512), jnp.bfloat16),
            pltpu.VMEM((256, 256), jnp.bfloat16),
            *weight_buffers(),
            pltpu.VMEM((4, 4, 64, 512), jnp.bfloat16),
            pltpu.SemaphoreType.DMA((32,)),
        ],
        compiler_params=pltpu.CompilerParams(vmem_limit_bytes=VMEM_LIMIT),
        cost_estimate=cost(4, 0),
        name=f"plain_{row}",
    )(patches, one_hot(token_order()), *weights)


def shifted_block(name, gather, scatter, ins, weights, wmerge, out, extra):
    count = len(gather)
    shapes = [merged_shape(8, 16), *extra]
    given = [] if out is None else [out]
    return pl.pallas_call(
        functools.partial(
            shifted_kernel, count, gather, scatter, len(ins), len(shapes), len(given)
        ),
        in_specs=[ANY] * (len(ins) + 6 + len(given)),
        out_specs=[ANY] * len(shapes),
        out_shape=shapes,
        input_output_aliases={len(ins) + 6: 0} if given else {},
        scratch_shapes=[
            pltpu.VMEM((count, 4, 64, 512), jnp.bfloat16),
            pltpu.VMEM((64, 64), jnp.bfloat16),
            *weight_buffers(),
            pltpu.VMEM((2048, 1024), jnp.bfloat16),
            pltpu.VMEM((count, 4, 4, 4, 1024), jnp.bfloat16),
            pltpu.VMEM((count, 4, 256, 128), jnp.float32),
            pltpu.SemaphoreType.DMA((40,)),
        ],
        compiler_params=pltpu.CompilerParams(vmem_limit_bytes=VMEM_LIMIT),
        cost_estimate=cost(count, 1),
        name=name,
    )(*ins, one_hot(merged_order()), *weights, wmerge, *given)


def shift(values, lat, lon, back):
    rows, cols = lax.axis_size("lat"), lax.axis_size("lon")
    pairs = []
    for i in range(rows):
        for j in range(cols):
            near, far = i * cols + j, (i + lat) % rows * cols + (j + lon) % cols
            pairs.append((far, near) if back else (near, far))
    return lax.ppermute(values, ("lat", "lon"), pairs)


def body(patches, qkv_weight, proj_weight, up_weight, down_weight, merge_weight):
    weights = (qkv_weight, proj_weight, up_weight, down_weight)
    up, corner, left_top, row1 = plain_block(0, patches, weights)
    up = shift(up, 1, 0, True)
    corner = shift(corner, 1, 1, True)
    left_top = shift(left_top, 0, 1, True)
    left_low, row2, row3 = plain_block(1, patches, weights)
    left_low = shift(left_low, 0, 1, True)
    near = [((0, 2 * w, 0, 2), (1, 2 * w, 2, 2)) for w in range(2)]
    put = [((0, 0, 0, 2, 2 + 4 * w, 4, 4),) for w in range(4)]
    (out,) = shifted_block("middle_ab", near, put[:2], (row1, row2), weights, merge_weight, None, [])
    edge = [((0, 2 * w, 0, 2), (1, 2 * w, 2, 2)) for w in range(3)]
    edge.append(((0, 6, 0, 1), (2, 1, 1, 1), (1, 6, 2, 1), (3, 0, 3, 1)))
    put_edge = [((0, 0, 0, 6, 2 + 4 * w, 2, 4), (1, 2, 0, 0, 4 * w, 2, 4)) for w in range(3)]
    put_edge.append(
        ((0, 0, 0, 6, 14, 2, 2), (3, 0, 2, 0, 0, 2, 2), (1, 2, 0, 0, 12, 2, 2), (2, 2, 2, 0, 0, 2, 2))
    )
    out, lat, diag, lon_low = shifted_block(
        "edge",
        edge,
        put_edge,
        (row3, up, left_low, corner),
        weights,
        merge_weight,
        out,
        [merged_shape(2, 14), merged_shape(2, 2), merged_shape(2, 2)],
    )
    lat = shift(lat, 1, 0, False)
    diag = shift(diag, 1, 1, False)
    lon_low = shift(lon_low, 0, 1, False)
    far = [
        ((0, 4, 0, 2), (1, 4, 2, 2)),
        ((0, 6, 0, 1), (2, 0, 1, 1), (1, 6, 2, 1), (3, 0, 3, 1)),
    ]
    put_far = [put[2], ((0, 0, 0, 2, 14, 4, 2), (1, 0, 2, 0, 0, 4, 2))]
    out, lon = shifted_block(
        "middle_cd",
        far,
        put_far,
        (row1, row2, left_top, left_low),
        weights,
        merge_weight,
        out,
        [merged_shape(4, 2)],
    )
    lon = shift(lon, 0, 1, False)
    return pl.pallas_call(
        finish_kernel,
        in_specs=[ANY] * 5,
        out_specs=ANY,
        out_shape=merged_shape(8, 16),
        input_output_aliases={4: 0},
        scratch_shapes=[pltpu.SemaphoreType.DMA((4,))],
        name="finish",
    )(lat, diag, lon_low, lon, out)


def solution(mesh):
    return jax.shard_map(
        body,
        mesh=mesh,
        in_specs=(P("lat", "lon", None, None), P(), P(), P(), P(), P()),
        out_specs=P("lat", "lon", None, None),
        check_vma=False,
    )
```

```python
import functools

import jax
import jax.numpy as jnp
from jax import lax
from jax.experimental import pallas as pl
from jax.experimental.pallas import tpu as pltpu
from jax.sharding import PartitionSpec as P
import numpy as np

HEADS = 8
PLAIN = ((0, 1), (2, 3))
SHIFTED = ((1, 2), (0, 3))
FFCHUNK = 2048
WEIGHTS = ((512, 1536), (512, 512), (512, 2048), (2048, 512))
VMEM_LIMIT = 56 * 1024 * 1024


def token_order():
    order = []
    for quarter_row in range(2):
        for quarter_col in range(2):
            for level in range(4):
                for r2 in range(2):
                    for c2 in range(2):
                        for q in range(4):
                            r = quarter_row * 4 + r2 * 2 + q % 2
                            c = quarter_col * 4 + c2 * 2 + q // 2
                            order.append((r * 8 + c) * 4 + level)
    return np.array(order)


def merged_order():
    order = []
    for r in range(4):
        for c in range(4):
            for level in range(4):
                order.append(((r // 2 * 2 + c // 2) * 4 + level) * 4 + (r % 2) * 2 + c % 2)
    return np.array(order)


def one_hot(order):
    return jnp.asarray(order[:, None] == np.arange(order.size)[None, :], jnp.bfloat16)


def normalize(values):
    centre = jnp.mean(values, axis=-1, keepdims=True)
    values = values - centre
    spread = jnp.mean(values * values, axis=-1, keepdims=True)
    return values * lax.rsqrt(spread + 1e-05)


def dot(a, b):
    return jnp.dot(a, b, preferred_element_type=jnp.float32)


def take_levels(values, levels):
    return jnp.concatenate(
        [values[t * 64 + lv * 16 : t * 64 + (lv + 1) * 16] for t in range(4) for lv in levels], axis=0
    )


def group_biases(cut):
    row = lax.broadcasted_iota(jnp.int32, (128, 128), 0)
    col = lax.broadcasted_iota(jnp.int32, (128, 128), 1)
    apart = (row // 16 % 2) != (col // 16 % 2)
    if cut is None:
        return None, jnp.where(apart, -1e30, 0.0)
    across = ((row // 64) != (col // 64)) & cut
    return jnp.where(across, -1e30, 0.0), jnp.where(across | apart, -1e30, 0.0)


def attend(qkv, groups, biases):
    outs = {}
    lane = lax.broadcasted_iota(jnp.int32, (128, 128), 1)
    even = jnp.where(lane < 64, 1.0, 0.0).astype(jnp.bfloat16)
    odd = jnp.where(lane < 64, 0.0, 1.0).astype(jnp.bfloat16)
    ones = jnp.concatenate([even, odd], axis=0)
    for levels, bias in zip(groups, biases):
        rows = take_levels(qkv, levels)
        pairs = []
        for p in range(4):
            q = rows[:, p * 128 : (p + 1) * 128]
            k = rows[:, 512 + p * 128 : 512 + (p + 1) * 128]
            v = rows[:, 1024 + p * 128 : 1024 + (p + 1) * 128]
            keys = jnp.concatenate([k * even, k * odd], axis=0)
            values = jnp.concatenate([v * even, v * odd], axis=0)
            values = jnp.concatenate([values, ones], axis=1)
            scores = lax.dot_general(
                q, keys, (((1,), (1,)), ((), ())), preferred_element_type=jnp.float32
            )
            halves = []
            for h in range(2):
                s = scores[:, h * 128 : (h + 1) * 128]
                if bias is not None:
                    s = s + bias
                highest = jnp.max(s, axis=-1, keepdims=True)
                halves.append(jnp.exp((s - highest) * 0.125).astype(jnp.bfloat16))
            out = dot(jnp.concatenate(halves, axis=1), values)
            pairs.append((out[:, :128] * (1.0 / out[:, 128:])).astype(jnp.bfloat16))
        out = jnp.concatenate(pairs, axis=1)
        for t in range(4):
            for n, lv in enumerate(levels):
                at = (t * len(levels) + n) * 16
                outs[t, lv] = out[at : at + 16]
    return jnp.concatenate([outs[t, lv] for t in range(4) for lv in range(4)], axis=0)


def gelu(x):
    half = 0.5 * x
    return half + half * jnp.tanh(x * (0.7978845608028654 + 0.035677408136300125 * (x * x)))


def block(streams, weights, groups, biases):
    normed = [normalize(s).astype(jnp.bfloat16) for s in streams]
    wqkv = weights[0]()
    for late in weights[1:]:
        late.begin()
    qkvs = [dot(n, wqkv[...]).astype(jnp.bfloat16) for n in normed]
    mixed = [attend(q, groups, b) for q, b in zip(qkvs, biases)]
    wproj = weights[1]()
    streams = [s + dot(m, wproj[...]) for s, m in zip(streams, mixed)]
    normed = [normalize(s).astype(jnp.bfloat16) for s in streams]
    hidden = [[] for _ in streams]
    wup = weights[2]()
    for c in range(0, 2048, FFCHUNK):
        for n, h in zip(normed, hidden):
            h.append(gelu(dot(n, wup[:, c : c + FFCHUNK])).astype(jnp.bfloat16))
    wdown = weights[3]()
    return [s + dot(jnp.concatenate(h, axis=1), wdown[...]) for s, h in zip(streams, hidden)]


class Late:
    def __init__(self, copies, source, target):
        self.copies, self.source, self.target, self.ready = copies, source, target, None

    def begin(self):
        if self.ready is None:
            self.ready = self.copies.later(self.source, self.target)

    def __call__(self):
        self.begin()
        return self.ready()


class Copies:
    def __init__(self, sems):
        self.sems, self.open = sems, []

    def start(self, source, target):
        copy = pltpu.make_async_copy(source, target, self.sems.at[len(self.open)])
        copy.start()
        self.open.append(copy)

    def wait(self, index):
        if self.open[index] is not None:
            self.open[index].wait()
            self.open[index] = None

    def later(self, source, target):
        index = len(self.open)
        self.start(source, target)

        def ready():
            self.wait(index)
            return target

        return ready

    def finish(self):
        for index in range(len(self.open)):
            self.wait(index)


def plain_kernel(windows, scatter, n_out, x_hbm, perm_hbm, wqkv, wproj, wup, wdown, *refs):
    outs, refs = refs[:n_out], refs[n_out:]
    x, perm, b0, b1, b2, b3, done, sems = refs
    copies = Copies(sems)
    order = copies.later(perm_hbm, perm)
    tokens = [
        copies.later(x_hbm.at[pl.ds(r * 8, 8), pl.ds(c * 8, 8)], x.at[w])
        for w, (r, c) in enumerate(windows)
    ]
    first = copies.later(wqkv.at[0], b0)
    streams = []
    for w in range(len(windows)):
        t = tokens[w]()[...].astype(jnp.float32).reshape(256, 512).astype(jnp.bfloat16)
        streams.append(dot(order()[...], t))
    weights = [first] + [Late(copies, s.at[0], d) for s, d in ((wproj, b1), (wup, b2), (wdown, b3))]
    streams = block(streams, weights, PLAIN, [(None, None)] * len(windows))
    for w in range(len(windows)):
        done[w] = streams[w].astype(jnp.bfloat16).reshape(4, 64, 512)
        for n, at, to, size in scatter[w]:
            copies.start(done.at[w, pl.ds(at, size)], outs[n].at[pl.ds(to, size)])
    copies.finish()


def merge(streams, perm, wmerge, scratch):
    for w, stream in enumerate(streams):
        for t in range(4):
            scratch[w, t] = stream[:, t * 128 : (t + 1) * 128]
    normed = []
    for w in range(len(streams)):
        pieces = [
            jnp.concatenate([scratch[w, t, pl.ds(q, 64, stride=4), :] for t in range(4)], axis=1)
            for q in range(4)
        ]
        normed.append(normalize(jnp.concatenate(pieces, axis=1)).astype(jnp.bfloat16))
    merged = dot(jnp.concatenate(normed, axis=0), wmerge()[...]).astype(jnp.bfloat16)
    return [dot(perm()[...], merged[w * 64 : (w + 1) * 64]) for w in range(len(streams))]


def shifted_kernel(count, edges, gather, scatter, n_in, n_out, aliased, *refs):
    ins, refs = refs[:n_in], refs[n_in:]
    perm_hbm, wqkv, wproj, wup, wdown, wmerge = refs[:6]
    refs = refs[6 + aliased :]
    outs, refs = refs[:n_out], refs[n_out:]
    x, perm, b0, b1, b2, b3, b4, done, scratch, sems = refs
    copies = Copies(sems)
    tokens = []
    for w in range(count):
        tokens.append(
            [
                copies.later(ins[n].at[pl.ds(at, size)], x.at[w, pl.ds(to, size)])
                for n, at, to, size in gather[w]
            ]
        )
    order = copies.later(perm_hbm, perm)
    first = copies.later(wqkv.at[1], b0)
    weights = [first] + [Late(copies, s.at[1], d) for s, d in ((wproj, b1), (wup, b2), (wdown, b3))]
    last = Late(copies, wmerge, b4)
    weights.append(last)
    plain = group_biases(None)
    if edges:
        cut = lax.axis_index("lat") == lax.axis_size("lat") - 1
        split = group_biases(cut)
    biases = [split if w < edges else plain for w in range(count)]
    streams = []
    for w in range(count):
        for piece in tokens[w]:
            piece()
        streams.append(x[w].reshape(256, 512).astype(jnp.float32))
    streams = block(streams, weights, SHIFTED, biases)
    rows = merge(streams, order, last, scratch)
    for w in range(count):
        done[w] = rows[w].reshape(4, 4, 4, 1024).astype(jnp.bfloat16)
        for n, r, c, to_r, to_c, size_r, size_c in scatter[w]:
            copies.start(
                done.at[w, pl.ds(r, size_r), pl.ds(c, size_c)],
                outs[n].at[pl.ds(to_r, size_r), pl.ds(to_c, size_c)],
            )
    copies.finish()


def finish_kernel(lat, diag, lon, partial, out, sems):
    copies = Copies(sems)
    copies.start(lat, out.at[pl.ds(0, 2), pl.ds(2, 14)])
    copies.start(diag, out.at[pl.ds(0, 2), pl.ds(0, 2)])
    copies.start(lon, out.at[pl.ds(2, 6), pl.ds(0, 2)])
    copies.finish()


ANY = pl.BlockSpec(memory_space=pl.ANY)
VMEM = pl.BlockSpec(memory_space=pltpu.VMEM)


def quarters(count):
    return jax.ShapeDtypeStruct((count, 64, 512), jnp.bfloat16)


def merged_shape(rows, cols):
    return jax.ShapeDtypeStruct((rows, cols, 4, 1024), jnp.bfloat16)


def weight_buffers():
    return [pltpu.VMEM(shape, jnp.bfloat16) for shape in WEIGHTS]


def cost(windows, merging):
    flops = windows * (2 * 256 * (512 * 6144) + 4 * 8 * 256 * 128 * 64)
    flops += windows * merging * 2 * 64 * 2048 * 1024
    return pl.CostEstimate(flops=flops, bytes_accessed=8 << 20, transcendentals=windows * 256 * 3072)


def plain_block(name, windows, scatter, shapes, patches, weights):
    count = len(windows)
    return pl.pallas_call(
        functools.partial(plain_kernel, windows, scatter, len(shapes)),
        in_specs=[ANY] * 6,
        out_specs=[ANY] * len(shapes),
        out_shape=shapes,
        scratch_shapes=[
            pltpu.VMEM((count, 8, 8, 4, 512), jnp.bfloat16),
            pltpu.VMEM((256, 256), jnp.bfloat16),
            *weight_buffers(),
            pltpu.VMEM((count, 4, 64, 512), jnp.bfloat16),
            pltpu.SemaphoreType.DMA((32,)),
        ],
        compiler_params=pltpu.CompilerParams(vmem_limit_bytes=VMEM_LIMIT),
        cost_estimate=cost(count, 0),
        name=name,
    )(patches, one_hot(token_order()), *weights)


def shifted_block(name, edges, gather, scatter, ins, specs, weights, wmerge, out, extra):
    count = len(gather)
    shapes = [merged_shape(8, 16), *extra]
    given = [] if out is None else [out]
    return pl.pallas_call(
        functools.partial(
            shifted_kernel, count, edges, gather, scatter, len(ins), len(shapes), len(given)
        ),
        in_specs=[*specs] + [ANY] * (6 + len(given)),
        out_specs=[ANY] * len(shapes),
        out_shape=shapes,
        input_output_aliases={len(ins) + 6: 0} if given else {},
        scratch_shapes=[
            pltpu.VMEM((count, 4, 64, 512), jnp.bfloat16),
            pltpu.VMEM((64, 64), jnp.bfloat16),
            *weight_buffers(),
            pltpu.VMEM((2048, 1024), jnp.bfloat16),
            pltpu.VMEM((count, 4, 4, 4, 1024), jnp.bfloat16),
            pltpu.VMEM((count, 4, 256, 128), jnp.float32),
            pltpu.SemaphoreType.DMA((48,)),
        ],
        compiler_params=pltpu.CompilerParams(vmem_limit_bytes=VMEM_LIMIT),
        cost_estimate=cost(count, 1),
        name=name,
    )(*ins, one_hot(merged_order()), *weights, wmerge, *given)


def shift(values, lat, lon, back):
    rows, cols = lax.axis_size("lat"), lax.axis_size("lon")
    pairs = []
    for i in range(rows):
        for j in range(cols):
            near, far = i * cols + j, (i + lat) % rows * cols + (j + lon) % cols
            pairs.append((far, near) if back else (near, far))
    return lax.ppermute(values, ("lat", "lon"), pairs)


def place(window):
    r, c = window
    if r == 0:
        if c == 0:
            return ((1, 0, 0, 1), (0, 1, 0, 1), (2, 2, 0, 1), (3, 3, 0, 1))
        return ((0, 0, 2 * c - 1, 2), (3, 2, 2 * c - 1, 2))
    if c == 0:
        return ((2, 0, 1, 1), (4, 1, 0, 1), (2, 2, 2, 1), (4, 3, 1, 1))
    return ((0, 0, 2 * c - 2, 2), (1, 2, 2 * c - 2, 2))


def body(patches, qkv_weight, proj_weight, up_weight, down_weight, merge_weight):
    weights = (qkv_weight, proj_weight, up_weight, down_weight)
    first = ((0, 0), (0, 1), (0, 2), (0, 3), (1, 0))
    second = ((1, 1), (1, 2), (1, 3))
    up, corner, left, row1, low = plain_block(
        "plain_sent",
        first,
        [place(w) for w in first],
        [quarters(7), quarters(1), quarters(3), quarters(7), quarters(2)],
        patches,
        weights,
    )
    up = shift(up, 1, 0, True)
    left = shift(left, 0, 1, True)
    corner = shift(corner, 1, 1, True)
    row2, row3 = plain_block(
        "plain_kept",
        second,
        [place(w) for w in second],
        [quarters(6), quarters(6)],
        patches,
        weights,
    )
    gather = [
        ((1, 1, 0, 1), (3, 0, 1, 1), (4, 0, 2, 2)),
        ((3, 1, 0, 2), (4, 2, 2, 2)),
        ((3, 3, 0, 2), (4, 4, 2, 2)),
        ((3, 5, 0, 1), (5, 2, 1, 1), (4, 6, 2, 1), (6, 0, 3, 1)),
        ((0, 6, 0, 1), (5, 0, 1, 1), (2, 5, 2, 1), (5, 1, 3, 1)),
    ]
    scatter = [((0, 0, 0, 6, 2 + 4 * w, 2, 4), (1, 2, 0, 0, 4 * w, 2, 4)) for w in range(3)]
    scatter.append(
        ((0, 0, 0, 6, 14, 2, 2), (3, 0, 2, 4, 0, 2, 2), (1, 2, 0, 0, 12, 2, 2), (2, 2, 2, 0, 0, 2, 2))
    )
    scatter.append(((0, 0, 0, 2, 14, 4, 2), (3, 0, 2, 0, 0, 4, 2)))
    out, lat, diag, lon = shifted_block(
        "shifted_sent",
        4,
        gather,
        scatter,
        (row1, low, row2, row3, up, left, corner),
        [ANY] * 4 + [VMEM] * 3,
        weights,
        merge_weight,
        None,
        [merged_shape(2, 14), merged_shape(2, 2), merged_shape(6, 2)],
    )
    lat = shift(lat, 1, 0, False)
    diag = shift(diag, 1, 1, False)
    lon = shift(lon, 0, 1, False)
    gather = [
        ((0, 0, 0, 2), (1, 0, 2, 1), (2, 0, 3, 1)),
        ((0, 2, 0, 2), (2, 1, 2, 2)),
        ((0, 4, 0, 2), (2, 3, 2, 2)),
    ]
    (out,) = shifted_block(
        "shifted_kept",
        0,
        gather,
        [((0, 0, 0, 2, 2 + 4 * w, 4, 4),) for w in range(3)],
        (row1, low, row2),
        [ANY] * 3,
        weights,
        merge_weight,
        out,
        [],
    )
    return pl.pallas_call(
        finish_kernel,
        in_specs=[VMEM] * 3 + [ANY],
        out_specs=ANY,
        out_shape=merged_shape(8, 16),
        input_output_aliases={3: 0},
        scratch_shapes=[pltpu.SemaphoreType.DMA((3,))],
        name="finish",
    )(lat, diag, lon, out)


def solution(mesh):
    return jax.shard_map(
        body,
        mesh=mesh,
        in_specs=(P("lat", "lon", None, None), P(), P(), P(), P(), P()),
        out_specs=P("lat", "lon", None, None),
        check_vma=False,
    )
```

```python
import functools

import jax
import jax.numpy as jnp
from jax import lax
from jax.experimental import pallas as pl
from jax.experimental.pallas import tpu as pltpu
from jax.sharding import PartitionSpec as P
import numpy as np

HEADS = 8
PLAIN = ((0, 1), (2, 3))
SHIFTED = ((1, 2), (0, 3))
FFCHUNK = 2048
WEIGHTS = ((512, 1536), (512, 2048), (2048, 512))
LIMITS = (39, 26, 30, 26, 4)


def normalize(values):
    centre = jnp.mean(values, axis=-1, keepdims=True)
    values = values - centre
    spread = jnp.mean(values * values, axis=-1, keepdims=True)
    return values * lax.rsqrt(spread + 1e-05)


def dot(a, b):
    return jnp.dot(a, b, preferred_element_type=jnp.float32)


def take_levels(values, levels):
    return jnp.concatenate(
        [values[t * 64 + lv * 16 : t * 64 + (lv + 1) * 16] for t in range(4) for lv in levels], axis=0
    )


def group_biases(cut):
    row = lax.broadcasted_iota(jnp.int32, (128, 128), 0)
    col = lax.broadcasted_iota(jnp.int32, (128, 128), 1)
    apart = (row // 16 % 2) != (col // 16 % 2)
    if cut is None:
        return None, jnp.where(apart, -1e30, 0.0)
    across = ((row // 64) != (col // 64)) & cut
    return jnp.where(across, -1e30, 0.0), jnp.where(across | apart, -1e30, 0.0)


def attend(qkv, groups, biases):
    outs = {}
    lane = lax.broadcasted_iota(jnp.int32, (128, 128), 1)
    even = jnp.where(lane < 64, 1.0, 0.0).astype(jnp.bfloat16)
    odd = jnp.where(lane < 64, 0.0, 1.0).astype(jnp.bfloat16)
    ones = jnp.concatenate([even, odd], axis=0)
    for levels, bias in zip(groups, biases):
        rows = take_levels(qkv, levels)
        pairs = []
        for p in range(4):
            q = rows[:, p * 128 : (p + 1) * 128]
            k = rows[:, 512 + p * 128 : 512 + (p + 1) * 128]
            v = rows[:, 1024 + p * 128 : 1024 + (p + 1) * 128]
            keys = jnp.concatenate([k * even, k * odd], axis=0)
            values = jnp.concatenate([v * even, v * odd], axis=0)
            values = jnp.concatenate([values, ones], axis=1)
            scores = lax.dot_general(
                q, keys, (((1,), (1,)), ((), ())), preferred_element_type=jnp.float32
            )
            halves = []
            for h in range(2):
                s = scores[:, h * 128 : (h + 1) * 128]
                if bias is not None:
                    s = s + bias
                highest = jnp.max(s, axis=-1, keepdims=True)
                halves.append(jnp.exp((s - highest) * 0.125).astype(jnp.bfloat16))
            out = dot(jnp.concatenate(halves, axis=1), values)
            pairs.append((out[:, :128] * (1.0 / out[:, 128:])).astype(jnp.bfloat16))
        out = jnp.concatenate(pairs, axis=1)
        for t in range(4):
            for n, lv in enumerate(levels):
                at = (t * len(levels) + n) * 16
                outs[t, lv] = out[at : at + 16]
    return jnp.concatenate([outs[t, lv] for t in range(4) for lv in range(4)], axis=0)


def gelu(x):
    half = 0.5 * x
    return half + half * jnp.tanh(x * (0.7978845608028654 + 0.035677408136300125 * (x * x)))


def block(streams, weights, groups, biases, ahead=()):
    normed = [normalize(s).astype(jnp.bfloat16) for s in streams]
    wqkv = weights[0]()
    for late in weights[1:]:
        late.begin()
    qkvs = [dot(n, wqkv[...]).astype(jnp.bfloat16) for n in normed]
    mixed = [attend(q, groups, b) for q, b in zip(qkvs, biases)]
    wproj = weights[1]()
    streams = [s + dot(m, wproj[...]) for s, m in zip(streams, mixed)]
    normed = [normalize(s).astype(jnp.bfloat16) for s in streams]
    hidden = [[] for _ in streams]
    wup = weights[2]()
    for late in ahead:
        late.begin()
    for c in range(0, 2048, FFCHUNK):
        for n, h in zip(normed, hidden):
            h.append(gelu(dot(n, wup[:, c : c + FFCHUNK])).astype(jnp.bfloat16))
    wdown = weights[3]()
    return [s + dot(jnp.concatenate(h, axis=1), wdown[...]) for s, h in zip(streams, hidden)]


class Held:
    def __init__(self, ref):
        self.ref = ref

    def begin(self):
        pass

    def __call__(self):
        return self.ref


class Late:
    def __init__(self, copies, source, target):
        self.copies, self.source, self.target, self.ready = copies, source, target, None

    def begin(self):
        if self.ready is None:
            self.ready = self.copies.later(self.source, self.target)

    def __call__(self):
        self.begin()
        return self.ready()


class Copies:
    def __init__(self, sems):
        self.sems, self.open = sems, []

    def start(self, source, target):
        copy = pltpu.make_async_copy(source, target, self.sems.at[len(self.open)])
        copy.start()
        self.open.append(copy)

    def wait(self, index):
        if self.open[index] is not None:
            self.open[index].wait()
            self.open[index] = None

    def later(self, source, target):
        index = len(self.open)
        self.start(source, target)

        def ready():
            self.wait(index)
            return target

        return ready

    def finish(self):
        for index in range(len(self.open)):
            self.wait(index)


def first_kernel(windows, scatter, x_hbm, proj, *refs):
    sources, outs, refs = refs[:3], refs[3:8], refs[8:]
    held, held_next, x, sems = refs[:3], refs[3:6], refs[6], refs[7]
    copies = Copies(sems)
    tokens = [
        copies.later(x_hbm.at[pl.ds(r * 8, 8), pl.ds(c * 8, 8)], x.at[w])
        for w, (r, c) in enumerate(windows)
    ]
    weights = [Late(copies, s.at[0], d) for s, d in zip(sources, held)]
    weights[0].begin()
    weights.insert(1, Held(proj.at[0]))
    ahead = [Late(copies, s.at[1], d) for s, d in zip(sources, held_next)]
    streams = ordered([lambda t=t: t()[...] for t in tokens])
    biases = [(None, None)] * len(windows)
    put_plain(block(streams, weights, PLAIN, biases, ahead), scatter, outs)
    copies.finish()


def second_kernel(windows, scatter, x, proj, wqkv, wup, wdown, *outs):
    weights = [Held(w) for w in (wqkv, proj.at[0], wup, wdown)]
    streams = ordered([lambda r=r, c=c: x[r * 8 : r * 8 + 8, c * 8 : c * 8 + 8] for r, c in windows])
    put_plain(block(streams, weights, PLAIN, [(None, None)] * len(windows)), scatter, outs)


def ordered(windows):
    row = lax.broadcasted_iota(jnp.int32, (256, 256), 0)
    col = lax.broadcasted_iota(jnp.int32, (256, 256), 1)
    quarter, level, inner, q = row // 64, row // 16 % 4, row // 4 % 4, row % 4
    r = quarter // 2 * 4 + inner // 2 * 2 + q % 2
    c = quarter % 2 * 4 + inner % 2 * 2 + q // 2
    order = jnp.where(col == (r * 8 + c) * 4 + level, 1.0, 0.0).astype(jnp.bfloat16)
    streams = []
    for window in windows:
        tokens = window().astype(jnp.float32)
        streams.append(dot(order, tokens.reshape(256, 512).astype(jnp.bfloat16)))
    return streams


def put_plain(streams, scatter, outs):
    for stream, pieces in zip(streams, scatter):
        done = stream.astype(jnp.bfloat16).reshape(4, 64, 512)
        for n, at, to, size in pieces:
            outs[n][to : to + size] = done[at : at + size]


def merge(streams, wmerge, scratch):
    for w, stream in enumerate(streams):
        for t in range(4):
            scratch[w, t] = stream[:, t * 128 : (t + 1) * 128]
    normed = []
    for w in range(len(streams)):
        pieces = [
            jnp.concatenate([scratch[w, t, pl.ds(q, 64, stride=4), :] for t in range(4)], axis=1)
            for q in range(4)
        ]
        normed.append(normalize(jnp.concatenate(pieces, axis=1)).astype(jnp.bfloat16))
    merged = dot(jnp.concatenate(normed, axis=0), wmerge[...]).astype(jnp.bfloat16)
    row = lax.broadcasted_iota(jnp.int32, (64, 64), 0)
    col = lax.broadcasted_iota(jnp.int32, (64, 64), 1)
    r, c, level = row // 16, row // 4 % 4, row % 4
    at = ((r // 2 * 2 + c // 2) * 4 + level) * 4 + r % 2 * 2 + c % 2
    order = jnp.where(col == at, 1.0, 0.0).astype(jnp.bfloat16)
    return [dot(order, merged[w * 64 : (w + 1) * 64]) for w in range(len(streams))]


def shifted_windows(count, edges, gather, ins, weights, wmerge, scratch):
    plain = group_biases(None)
    if edges:
        cut = lax.axis_index("lat") == lax.axis_size("lat") - 1
        split = group_biases(cut)
    biases = [split if w < edges else plain for w in range(count)]
    streams = []
    for w in range(count):
        pieces = [ins[n][at : at + size] for n, at, size in gather[w]]
        streams.append(jnp.concatenate(pieces, axis=0).reshape(256, 512).astype(jnp.float32))
    weights = [Held(w) for w in weights]
    streams = block(streams, weights, SHIFTED, biases)
    rows = merge(streams, wmerge, scratch)
    return [r.reshape(4, 4, 4, 1024).astype(jnp.bfloat16) for r in rows]


def third_kernel(gather, scatter, n_in, n_out, *refs):
    ins, refs = refs[:n_in], refs[n_in:]
    proj, *weights, wmerge = refs[:5]
    weights.insert(1, proj.at[1])
    outs, scratch = refs[5 : 5 + n_out], refs[5 + n_out]
    rows = shifted_windows(len(gather), 4, gather, ins, weights, wmerge, scratch)
    for w, done in enumerate(rows):
        for n, r, c, to_r, to_c, size_r, size_c in scatter[w]:
            outs[n][to_r : to_r + size_r, to_c : to_c + size_c] = done[r : r + size_r, c : c + size_c]


def fourth_kernel(gather, n_in, edge, side, *refs):
    ins, refs = refs[:n_in], refs[n_in:]
    proj, *weights, wmerge, out, scratch, done, sems = refs
    weights.insert(1, proj.at[1])
    copies = Copies(sems)
    copies.start(edge, out.at[pl.ds(6, 2), pl.ds(2, 14)])
    copies.start(side, out.at[pl.ds(2, 4), pl.ds(14, 2)])
    rows = shifted_windows(len(gather), 0, gather, ins, weights, wmerge, scratch)
    for w, row in enumerate(rows):
        done[w] = row
        copies.start(done.at[w], out.at[pl.ds(2, 4), pl.ds(2 + 4 * w, 4)])
    copies.finish()


def finish_kernel(lat, diag, lon, partial, out, sems):
    copies = Copies(sems)
    copies.start(lat, out.at[pl.ds(0, 2), pl.ds(2, 14)])
    copies.start(diag, out.at[pl.ds(0, 2), pl.ds(0, 2)])
    copies.start(lon, out.at[pl.ds(2, 6), pl.ds(0, 2)])
    copies.finish()


ANY = pl.BlockSpec(memory_space=pl.ANY)
VMEM = pl.BlockSpec(memory_space=pltpu.VMEM)
HBM = pl.BlockSpec(memory_space=pltpu.HBM)


def quarters(count):
    return jax.ShapeDtypeStruct((count, 64, 512), jnp.bfloat16)


def merged_shape(rows, cols):
    return jax.ShapeDtypeStruct((rows, cols, 4, 1024), jnp.bfloat16)


def cost(windows, merging):
    flops = windows * (2 * 256 * (512 * 6144) + 4 * 8 * 256 * 128 * 64)
    flops += windows * merging * 2 * 64 * 2048 * 1024
    return pl.CostEstimate(flops=flops, bytes_accessed=8 << 20, transcendentals=windows * 256 * 3072)


def shift(values, lat, lon, back):
    rows, cols = lax.axis_size("lat"), lax.axis_size("lon")
    pairs = []
    for i in range(rows):
        for j in range(cols):
            near, far = i * cols + j, (i + lat) % rows * cols + (j + lon) % cols
            pairs.append((far, near) if back else (near, far))
    return lax.ppermute(values, ("lat", "lon"), pairs)


def place(window):
    r, c = window
    if r == 0:
        if c == 0:
            return ((1, 0, 0, 1), (0, 1, 0, 1), (2, 2, 0, 1), (3, 3, 0, 1))
        return ((0, 0, 2 * c - 1, 2), (3, 2, 2 * c - 1, 2))
    if c == 0:
        return ((2, 0, 1, 1), (4, 1, 0, 1), (2, 2, 2, 1), (4, 3, 1, 1))
    return ((0, 0, 2 * c - 2, 2), (1, 2, 2 * c - 2, 2))


def place(window):
    r, c = window
    if r == 0:
        if c == 0:
            return ((1, 0, 0, 1), (0, 1, 0, 1), (2, 2, 0, 1), (3, 3, 0, 1))
        return ((0, 0, 2 * c - 1, 2), (3, 2, 2 * c - 1, 2))
    if c == 0:
        return ((2, 0, 1, 1), (4, 1, 0, 1), (2, 2, 2, 1), (4, 3, 1, 1))
    return ((0, 0, 2 * c - 2, 2), (1, 2, 2 * c - 2, 2))


def merge_scratch(count):
    return pltpu.VMEM((count, 4, 256, 128), jnp.float32)


def params(limit):
    return pltpu.CompilerParams(vmem_limit_bytes=limit << 20)


def body(patches, qkv_weight, proj_weight, up_weight, down_weight, merge_weight):
    first = ((0, 0), (0, 1), (0, 2), (0, 3), (1, 0))
    second = ((1, 1), (1, 2), (1, 3))
    held = [jax.ShapeDtypeStruct(shape, jnp.bfloat16) for shape in WEIGHTS]
    up, corner, left, row1, low, *held = pl.pallas_call(
        functools.partial(first_kernel, first, [place(w) for w in first]),
        in_specs=[HBM, VMEM] + [HBM] * 3,
        out_specs=[VMEM] * 11,
        out_shape=[quarters(7), quarters(1), quarters(3), quarters(7), quarters(2), *held, *held],
        scratch_shapes=[
            pltpu.VMEM((5, 8, 8, 4, 512), jnp.bfloat16),
            pltpu.SemaphoreType.DMA((16,)),
        ],
        compiler_params=params(LIMITS[0]),
        cost_estimate=cost(5, 0),
        name="plain_sent",
    )(patches, proj_weight, qkv_weight, up_weight, down_weight)
    weights, weights_next = held[:3], held[3:]
    up = shift(up, 1, 0, True)
    left = shift(left, 0, 1, True)
    corner = shift(corner, 1, 1, True)
    row2, row3 = pl.pallas_call(
        functools.partial(second_kernel, second, [place(w) for w in second]),
        in_specs=[VMEM] * 5,
        out_specs=[VMEM] * 2,
        out_shape=[quarters(6), quarters(6)],
        compiler_params=params(LIMITS[1]),
        cost_estimate=cost(3, 0),
        name="plain_kept",
    )(patches, proj_weight, *weights)
    gather = [
        ((1, 1, 1), (3, 0, 1), (4, 0, 2)),
        ((3, 1, 2), (4, 2, 2)),
        ((3, 3, 2), (4, 4, 2)),
        ((3, 5, 1), (5, 2, 1), (4, 6, 1), (6, 0, 1)),
        ((0, 6, 1), (5, 0, 1), (2, 5, 1), (5, 1, 1)),
    ]
    scatter = [((0, 0, 0, 0, 4 * w, 2, 4), (1, 2, 0, 0, 4 * w, 2, 4)) for w in range(3)]
    scatter.append(
        ((0, 0, 0, 0, 12, 2, 2), (3, 0, 2, 4, 0, 2, 2), (1, 2, 0, 0, 12, 2, 2), (2, 2, 2, 0, 0, 2, 2))
    )
    scatter.append(((4, 0, 0, 0, 0, 4, 2), (3, 0, 2, 0, 0, 4, 2)))
    edge, lat, diag, lon, side = pl.pallas_call(
        functools.partial(third_kernel, gather, scatter, 7, 5),
        in_specs=[VMEM] * 12,
        out_specs=[VMEM] * 5,
        out_shape=[
            merged_shape(2, 14),
            merged_shape(2, 14),
            merged_shape(2, 2),
            merged_shape(6, 2),
            merged_shape(4, 2),
        ],
        scratch_shapes=[merge_scratch(5)],
        compiler_params=params(LIMITS[2]),
        cost_estimate=cost(5, 1),
        name="shifted_sent",
    )(row1, low, row2, row3, up, left, corner, proj_weight, *weights_next, merge_weight)
    lat = shift(lat, 1, 0, False)
    diag = shift(diag, 1, 1, False)
    lon = shift(lon, 0, 1, False)
    gather = [
        ((0, 0, 2), (1, 0, 1), (2, 0, 1)),
        ((0, 2, 2), (2, 1, 2)),
        ((0, 4, 2), (2, 3, 2)),
    ]
    out = pl.pallas_call(
        functools.partial(fourth_kernel, gather, 3),
        in_specs=[VMEM] * 10,
        out_specs=HBM,
        out_shape=merged_shape(8, 16),
        scratch_shapes=[
            merge_scratch(3),
            pltpu.VMEM((3, 4, 4, 4, 1024), jnp.bfloat16),
            pltpu.SemaphoreType.DMA((5,)),
        ],
        compiler_params=params(LIMITS[3]),
        cost_estimate=cost(3, 1),
        name="shifted_kept",
    )(edge, side, row1, low, row2, proj_weight, *weights_next, merge_weight)
    return pl.pallas_call(
        finish_kernel,
        in_specs=[VMEM] * 3 + [HBM],
        out_specs=HBM,
        out_shape=merged_shape(8, 16),
        input_output_aliases={3: 0},
        scratch_shapes=[pltpu.SemaphoreType.DMA((3,))],
        compiler_params=params(LIMITS[4]),
        name="finish",
    )(lat, diag, lon, out)


def solution(mesh):
    return jax.shard_map(
        body,
        mesh=mesh,
        in_specs=(P("lat", "lon", None, None), P(), P(), P(), P(), P()),
        out_specs=P("lat", "lon", None, None),
        check_vma=False,
    )
```

```python
import functools

import jax
import jax.numpy as jnp
from jax import lax
from jax.experimental import pallas as pl
from jax.experimental.pallas import tpu as pltpu
from jax.sharding import PartitionSpec as P
import numpy as np

HEADS = 8
PLAIN = ((0, 1), (2, 3))
SHIFTED = ((1, 2), (0, 3))
FFCHUNK = 2048
WEIGHTS = ((512, 1536), (512, 512), (512, 2048), (2048, 512))
LIMITS = (38, 26, 30, 26, 4)


def normalize(values):
    centre = jnp.mean(values, axis=-1, keepdims=True)
    values = values - centre
    spread = jnp.mean(values * values, axis=-1, keepdims=True)
    return values * lax.rsqrt(spread + 1e-05)


def dot(a, b):
    return jnp.dot(a, b, preferred_element_type=jnp.float32)


def take_levels(values, levels):
    return jnp.concatenate(
        [values[t * 64 + lv * 16 : t * 64 + (lv + 1) * 16] for t in range(4) for lv in levels], axis=0
    )


def group_biases(cut):
    row = lax.broadcasted_iota(jnp.int32, (128, 128), 0)
    col = lax.broadcasted_iota(jnp.int32, (128, 128), 1)
    apart = (row // 16 % 2) != (col // 16 % 2)
    if cut is None:
        return None, jnp.where(apart, -1e30, 0.0)
    across = ((row // 64) != (col // 64)) & cut
    return jnp.where(across, -1e30, 0.0), jnp.where(across | apart, -1e30, 0.0)


def attend(qkv, groups, biases):
    outs = {}
    lane = lax.broadcasted_iota(jnp.int32, (128, 128), 1)
    even = jnp.where(lane < 64, 1.0, 0.0).astype(jnp.bfloat16)
    odd = jnp.where(lane < 64, 0.0, 1.0).astype(jnp.bfloat16)
    ones = jnp.concatenate([even, odd], axis=0)
    for levels, bias in zip(groups, biases):
        rows = take_levels(qkv, levels)
        pairs = []
        for p in range(4):
            q = rows[:, p * 128 : (p + 1) * 128]
            k = rows[:, 512 + p * 128 : 512 + (p + 1) * 128]
            v = rows[:, 1024 + p * 128 : 1024 + (p + 1) * 128]
            keys = jnp.concatenate([k * even, k * odd], axis=0)
            values = jnp.concatenate([v * even, v * odd], axis=0)
            values = jnp.concatenate([values, ones], axis=1)
            scores = lax.dot_general(
                q, keys, (((1,), (1,)), ((), ())), preferred_element_type=jnp.float32
            )
            halves = []
            for h in range(2):
                s = scores[:, h * 128 : (h + 1) * 128]
                if bias is not None:
                    s = s + bias
                highest = jnp.max(s, axis=-1, keepdims=True)
                halves.append(jnp.exp((s - highest) * 0.125).astype(jnp.bfloat16))
            out = dot(jnp.concatenate(halves, axis=1), values)
            pairs.append((out[:, :128] * (1.0 / out[:, 128:])).astype(jnp.bfloat16))
        out = jnp.concatenate(pairs, axis=1)
        for t in range(4):
            for n, lv in enumerate(levels):
                at = (t * len(levels) + n) * 16
                outs[t, lv] = out[at : at + 16]
    return jnp.concatenate([outs[t, lv] for t in range(4) for lv in range(4)], axis=0)


def gelu(x):
    x = x.astype(jnp.bfloat16)
    half = 0.5 * x
    return half + half * jnp.tanh(x * (0.7978845608028654 + 0.035677408136300125 * (x * x)))


def block(streams, weights, groups, biases, ahead=()):
    normed = [normalize(s).astype(jnp.bfloat16) for s in streams]
    wqkv = weights[0]()
    for late in weights[1:]:
        late.begin()
    qkvs = [dot(n, wqkv[...]).astype(jnp.bfloat16) for n in normed]
    mixed = [attend(q, groups, b) for q, b in zip(qkvs, biases)]
    wproj = weights[1]()
    streams = [s + dot(m, wproj[...]) for s, m in zip(streams, mixed)]
    normed = [normalize(s).astype(jnp.bfloat16) for s in streams]
    hidden = [[] for _ in streams]
    wup = weights[2]()
    for late in ahead:
        late.begin()
    for c in range(0, 2048, FFCHUNK):
        for n, h in zip(normed, hidden):
            h.append(gelu(dot(n, wup[:, c : c + FFCHUNK])).astype(jnp.bfloat16))
    wdown = weights[3]()
    return [s + dot(jnp.concatenate(h, axis=1), wdown[...]) for s, h in zip(streams, hidden)]


class Held:
    def __init__(self, ref):
        self.ref = ref

    def begin(self):
        pass

    def __call__(self):
        return self.ref


class Late:
    def __init__(self, copies, source, target):
        self.copies, self.source, self.target, self.ready = copies, source, target, None

    def begin(self):
        if self.ready is None:
            self.ready = self.copies.later(self.source, self.target)

    def __call__(self):
        self.begin()
        return self.ready()


class Copies:
    def __init__(self, sems):
        self.sems, self.open = sems, []

    def start(self, source, target):
        copy = pltpu.make_async_copy(source, target, self.sems.at[len(self.open)])
        copy.start()
        self.open.append(copy)

    def wait(self, index):
        if self.open[index] is not None:
            self.open[index].wait()
            self.open[index] = None

    def later(self, source, target):
        index = len(self.open)
        self.start(source, target)

        def ready():
            self.wait(index)
            return target

        return ready

    def finish(self):
        for index in range(len(self.open)):
            self.wait(index)


def first_kernel(scatter, x_hbm, *refs):
    sources, outs, refs = refs[:4], refs[4:8], refs[8:]
    x_next, held, held_next, x, sems = refs[0], refs[1:5], refs[5:9], refs[9], refs[10]
    copies = Copies(sems)
    tokens = [
        copies.later(x_hbm.at[pl.ds(0, 8), pl.ds(w * 8, 8)], x.at[w]) for w in range(4)
    ]
    weights = [Late(copies, s.at[0], d) for s, d in zip(sources, held)]
    weights[0].begin()
    ahead = [Late(copies, x_hbm.at[pl.ds(8, 8), pl.ds(w * 8, 8)], x_next.at[w]) for w in range(4)]
    ahead += [Late(copies, s.at[1], d) for s, d in zip(sources, held_next)]
    streams = ordered([lambda t=t: t()[...] for t in tokens])
    put_plain(block(streams, weights, PLAIN, [(None, None)] * 4, ahead), scatter, outs)
    copies.finish()


def second_kernel(scatter, x, side, wqkv, wproj, wup, wdown, *outs):
    outs[0][0:1] = side[...]
    weights = [Held(w) for w in (wqkv, wproj, wup, wdown)]
    streams = ordered([lambda w=w: x[w] for w in range(4)])
    put_plain(block(streams, weights, PLAIN, [(None, None)] * 4), scatter, outs)


def ordered(windows):
    row = lax.broadcasted_iota(jnp.int32, (256, 256), 0)
    col = lax.broadcasted_iota(jnp.int32, (256, 256), 1)
    quarter, level, inner, q = row // 64, row // 16 % 4, row // 4 % 4, row % 4
    r = quarter // 2 * 4 + inner // 2 * 2 + q % 2
    c = quarter % 2 * 4 + inner % 2 * 2 + q // 2
    order = jnp.where(col == (r * 8 + c) * 4 + level, 1.0, 0.0).astype(jnp.bfloat16)
    streams = []
    for window in windows:
        tokens = window().astype(jnp.float32)
        streams.append(dot(order, tokens.reshape(256, 512).astype(jnp.bfloat16)))
    return streams


def put_plain(streams, scatter, outs):
    for stream, pieces in zip(streams, scatter):
        done = stream.astype(jnp.bfloat16).reshape(4, 64, 512)
        for n, at, to, size in pieces:
            outs[n][to : to + size] = done[at : at + size]


def merge(streams, wmerge, scratch):
    for w, stream in enumerate(streams):
        for t in range(4):
            scratch[w, t] = stream[:, t * 128 : (t + 1) * 128]
    normed = []
    for w in range(len(streams)):
        pieces = [
            jnp.concatenate([scratch[w, t, pl.ds(q, 64, stride=4), :] for t in range(4)], axis=1)
            for q in range(4)
        ]
        normed.append(normalize(jnp.concatenate(pieces, axis=1)).astype(jnp.bfloat16))
    merged = dot(jnp.concatenate(normed, axis=0), wmerge[...]).astype(jnp.bfloat16)
    row = lax.broadcasted_iota(jnp.int32, (64, 64), 0)
    col = lax.broadcasted_iota(jnp.int32, (64, 64), 1)
    r, c, level = row // 16, row // 4 % 4, row % 4
    at = ((r // 2 * 2 + c // 2) * 4 + level) * 4 + r % 2 * 2 + c % 2
    order = jnp.where(col == at, 1.0, 0.0).astype(jnp.bfloat16)
    return [dot(order, merged[w * 64 : (w + 1) * 64]) for w in range(len(streams))]


def shifted_windows(count, edges, gather, ins, weights, wmerge, scratch):
    plain = group_biases(None)
    if edges:
        cut = lax.axis_index("lat") == lax.axis_size("lat") - 1
        split = group_biases(cut)
    biases = [split if w < edges else plain for w in range(count)]
    streams = []
    for w in range(count):
        pieces = [ins[n][at : at + size] for n, at, size in gather[w]]
        streams.append(jnp.concatenate(pieces, axis=0).reshape(256, 512).astype(jnp.float32))
    weights = [Held(w) for w in weights]
    streams = block(streams, weights, SHIFTED, biases)
    rows = merge(streams, wmerge, scratch)
    return [r.reshape(4, 4, 4, 1024).astype(jnp.bfloat16) for r in rows]


def third_kernel(gather, scatter, n_in, n_out, *refs):
    ins, refs = refs[:n_in], refs[n_in:]
    *weights, wmerge = refs[:5]
    outs, scratch = refs[5 : 5 + n_out], refs[5 + n_out]
    rows = shifted_windows(len(gather), 4, gather, ins, weights, wmerge, scratch)
    for w, done in enumerate(rows):
        for n, r, c, to_r, to_c, size_r, size_c in scatter[w]:
            outs[n][to_r : to_r + size_r, to_c : to_c + size_c] = done[r : r + size_r, c : c + size_c]


def fourth_kernel(gather, n_in, edge, side, *refs):
    ins, refs = refs[:n_in], refs[n_in:]
    *weights, wmerge, out, scratch, done, sems = refs
    copies = Copies(sems)
    copies.start(edge, out.at[pl.ds(6, 2), pl.ds(2, 14)])
    copies.start(side, out.at[pl.ds(2, 4), pl.ds(14, 2)])
    rows = shifted_windows(len(gather), 0, gather, ins, weights, wmerge, scratch)
    for w, row in enumerate(rows):
        done[w] = row
        copies.start(done.at[w], out.at[pl.ds(2, 4), pl.ds(2 + 4 * w, 4)])
    copies.finish()


def finish_kernel(lat, diag, lon, partial, out, sems):
    copies = Copies(sems)
    copies.start(lat, out.at[pl.ds(0, 2), pl.ds(2, 14)])
    copies.start(diag, out.at[pl.ds(0, 2), pl.ds(0, 2)])
    copies.start(lon, out.at[pl.ds(2, 6), pl.ds(0, 2)])
    copies.finish()


ANY = pl.BlockSpec(memory_space=pl.ANY)
VMEM = pl.BlockSpec(memory_space=pltpu.VMEM)
HBM = pl.BlockSpec(memory_space=pltpu.HBM)


def quarters(count):
    return jax.ShapeDtypeStruct((count, 64, 512), jnp.bfloat16)


def merged_shape(rows, cols):
    return jax.ShapeDtypeStruct((rows, cols, 4, 1024), jnp.bfloat16)


def cost(windows, merging):
    flops = windows * (2 * 256 * (512 * 6144) + 4 * 8 * 256 * 128 * 64)
    flops += windows * merging * 2 * 64 * 2048 * 1024
    return pl.CostEstimate(flops=flops, bytes_accessed=8 << 20, transcendentals=windows * 256 * 3072)


def shift(values, lat, lon, back):
    rows, cols = lax.axis_size("lat"), lax.axis_size("lon")
    pairs = []
    for i in range(rows):
        for j in range(cols):
            near, far = i * cols + j, (i + lat) % rows * cols + (j + lon) % cols
            pairs.append((far, near) if back else (near, far))
    return lax.ppermute(values, ("lat", "lon"), pairs)


def merge_scratch(count):
    return pltpu.VMEM((count, 4, 256, 128), jnp.float32)


def params(limit):
    return pltpu.CompilerParams(vmem_limit_bytes=limit << 20)


def body(patches, qkv_weight, proj_weight, up_weight, down_weight, merge_weight):
    sources = (qkv_weight, proj_weight, up_weight, down_weight)
    held = [jax.ShapeDtypeStruct(shape, jnp.bfloat16) for shape in WEIGHTS]
    scatter = [((3, 0, 0, 1), (0, 1, 0, 1), (2, 2, 0, 1), (1, 3, 0, 1))]
    scatter += [((0, 0, 2 * c - 1, 2), (1, 2, 2 * c - 1, 2)) for c in range(1, 4)]
    up, row1, side, corner, x_next, *held = pl.pallas_call(
        functools.partial(first_kernel, scatter),
        in_specs=[HBM] * 5,
        out_specs=[VMEM] * 13,
        out_shape=[
            quarters(7),
            quarters(7),
            quarters(1),
            quarters(1),
            jax.ShapeDtypeStruct((4, 8, 8, 4, 512), jnp.bfloat16),
            *held,
            *held,
        ],
        scratch_shapes=[
            pltpu.VMEM((4, 8, 8, 4, 512), jnp.bfloat16),
            pltpu.SemaphoreType.DMA((16,)),
        ],
        compiler_params=params(LIMITS[0]),
        cost_estimate=cost(4, 0),
        name="plain_upper",
    )(patches, *sources)
    up = shift(up, 1, 0, True)
    corner = shift(corner, 1, 1, True)
    scatter = [((0, 0, 1, 1), (1, 1, 0, 1), (0, 2, 2, 1), (2, 3, 0, 1))]
    scatter += [((1, 0, 2 * c - 1, 2), (2, 2, 2 * c - 1, 2)) for c in range(1, 4)]
    left, row2, row3 = pl.pallas_call(
        functools.partial(second_kernel, scatter),
        in_specs=[VMEM] * 6,
        out_specs=[VMEM] * 3,
        out_shape=[quarters(3), quarters(7), quarters(7)],
        compiler_params=params(LIMITS[1]),
        cost_estimate=cost(4, 0),
        name="plain_lower",
    )(x_next, side, *held[:4])
    weights_next = held[4:]
    left = shift(left, 0, 1, True)
    gather = [((2, 2 * w, 2), (3, 2 * w, 2)) for w in range(3)]
    gather.append(((2, 6, 1), (4, 2, 1), (3, 6, 1), (5, 0, 1)))
    gather.append(((0, 6, 1), (4, 0, 1), (1, 6, 1), (4, 1, 1)))
    scatter = [((0, 0, 0, 0, 4 * w, 2, 4), (1, 2, 0, 0, 4 * w, 2, 4)) for w in range(3)]
    scatter.append(
        ((0, 0, 0, 0, 12, 2, 2), (3, 0, 2, 4, 0, 2, 2), (1, 2, 0, 0, 12, 2, 2), (2, 2, 2, 0, 0, 2, 2))
    )
    scatter.append(((4, 0, 0, 0, 0, 4, 2), (3, 0, 2, 0, 0, 4, 2)))
    edge, lat, diag, lon, side = pl.pallas_call(
        functools.partial(third_kernel, gather, scatter, 6, 5),
        in_specs=[VMEM] * 11,
        out_specs=[VMEM] * 5,
        out_shape=[
            merged_shape(2, 14),
            merged_shape(2, 14),
            merged_shape(2, 2),
            merged_shape(6, 2),
            merged_shape(4, 2),
        ],
        scratch_shapes=[merge_scratch(5)],
        compiler_params=params(LIMITS[2]),
        cost_estimate=cost(5, 1),
        name="shifted_sent",
    )(row1, row2, row3, up, left, corner, *weights_next, merge_weight)
    lat = shift(lat, 1, 0, False)
    diag = shift(diag, 1, 1, False)
    lon = shift(lon, 0, 1, False)
    gather = [((0, 2 * w, 2), (1, 2 * w, 2)) for w in range(3)]
    out = pl.pallas_call(
        functools.partial(fourth_kernel, gather, 2),
        in_specs=[VMEM] * 9,
        out_specs=HBM,
        out_shape=merged_shape(8, 16),
        scratch_shapes=[
            merge_scratch(3),
            pltpu.VMEM((3, 4, 4, 4, 1024), jnp.bfloat16),
            pltpu.SemaphoreType.DMA((5,)),
        ],
        compiler_params=params(LIMITS[3]),
        cost_estimate=cost(3, 1),
        name="shifted_kept",
    )(edge, side, row1, row2, *weights_next, merge_weight)
    return pl.pallas_call(
        finish_kernel,
        in_specs=[VMEM] * 3 + [HBM],
        out_specs=HBM,
        out_shape=merged_shape(8, 16),
        input_output_aliases={3: 0},
        scratch_shapes=[pltpu.SemaphoreType.DMA((3,))],
        compiler_params=params(LIMITS[4]),
        name="finish",
    )(lat, diag, lon, out)


def solution(mesh):
    return jax.shard_map(
        body,
        mesh=mesh,
        in_specs=(P("lat", "lon", None, None), P(), P(), P(), P(), P()),
        out_specs=P("lat", "lon", None, None),
        check_vma=False,
    )
```

```python
import functools

import jax
import jax.numpy as jnp
from jax import lax
from jax.experimental import pallas as pl
from jax.experimental.pallas import tpu as pltpu
from jax.sharding import PartitionSpec as P
import numpy as np

HEADS = 8
PLAIN = ((0, 1), (2, 3))
SHIFTED = ((1, 2), (0, 3))
FFCHUNK = 2048
WEIGHTS = ((512, 1536), (512, 512), (512, 2048), (2048, 512))
LIMITS = (38, 26, 30, 26, 4)


def normalize(values):
    centre = jnp.mean(values, axis=-1, keepdims=True)
    values = values - centre
    spread = jnp.mean(values * values, axis=-1, keepdims=True)
    return values * lax.rsqrt(spread + 1e-05)


def dot(a, b):
    return jnp.dot(a, b, preferred_element_type=jnp.float32)


def take_levels(values, levels):
    return jnp.concatenate(
        [values[t * 64 + lv * 16 : t * 64 + (lv + 1) * 16] for t in range(4) for lv in levels], axis=0
    )


def group_biases(cut):
    row = lax.broadcasted_iota(jnp.int32, (128, 128), 0)
    col = lax.broadcasted_iota(jnp.int32, (128, 128), 1)
    apart = (row // 16 % 2) != (col // 16 % 2)
    if cut is None:
        return None, jnp.where(apart, -1e30, 0.0)
    across = ((row // 64) != (col // 64)) & cut
    return jnp.where(across, -1e30, 0.0), jnp.where(across | apart, -1e30, 0.0)


def attend(qkv, groups, biases):
    outs = {}
    lane = lax.broadcasted_iota(jnp.int32, (128, 128), 1)
    even = jnp.where(lane < 64, 1.0, 0.0).astype(jnp.bfloat16)
    odd = jnp.where(lane < 64, 0.0, 1.0).astype(jnp.bfloat16)
    ones = jnp.concatenate([even, odd], axis=0)
    for levels, bias in zip(groups, biases):
        rows = take_levels(qkv, levels)
        pairs = []
        for p in range(4):
            q = rows[:, p * 128 : (p + 1) * 128]
            k = rows[:, 512 + p * 128 : 512 + (p + 1) * 128]
            v = rows[:, 1024 + p * 128 : 1024 + (p + 1) * 128]
            keys = jnp.concatenate([k * even, k * odd], axis=0)
            values = jnp.concatenate([v * even, v * odd], axis=0)
            values = jnp.concatenate([values, ones], axis=1)
            scores = lax.dot_general(
                q, keys, (((1,), (1,)), ((), ())), preferred_element_type=jnp.float32
            )
            halves = []
            for h in range(2):
                s = scores[:, h * 128 : (h + 1) * 128]
                if bias is not None:
                    s = s + bias
                highest = jnp.max(s, axis=-1, keepdims=True)
                halves.append(jnp.exp((s - highest) * 0.125).astype(jnp.bfloat16))
            out = dot(jnp.concatenate(halves, axis=1), values)
            pairs.append((out[:, :128] * (1.0 / out[:, 128:])).astype(jnp.bfloat16))
        out = jnp.concatenate(pairs, axis=1)
        for t in range(4):
            for n, lv in enumerate(levels):
                at = (t * len(levels) + n) * 16
                outs[t, lv] = out[at : at + 16]
    return jnp.concatenate([outs[t, lv] for t in range(4) for lv in range(4)], axis=0)


def gelu(x):
    x = x.astype(jnp.bfloat16)
    half = 0.5 * x
    return half + half * jnp.tanh(x * (0.7978845608028654 + 0.035677408136300125 * (x * x)))


def block(streams, weights, groups, biases, ahead=()):
    normed = [normalize(s).astype(jnp.bfloat16) for s in streams]
    wqkv = weights[0]()
    for late in weights[1:]:
        late.begin()
    qkvs = [dot(n, wqkv[...]).astype(jnp.bfloat16) for n in normed]
    mixed = [attend(q, groups, b) for q, b in zip(qkvs, biases)]
    wproj = weights[1]()
    for late in ahead:
        late.begin()
    streams = [s + dot(m, wproj[...]) for s, m in zip(streams, mixed)]
    normed = [normalize(s).astype(jnp.bfloat16) for s in streams]
    hidden = [[] for _ in streams]
    wup = weights[2]()
    for c in range(0, 2048, FFCHUNK):
        for n, h in zip(normed, hidden):
            h.append(gelu(dot(n, wup[:, c : c + FFCHUNK])).astype(jnp.bfloat16))
    wdown = weights[3]()
    return [s + dot(jnp.concatenate(h, axis=1), wdown[...]) for s, h in zip(streams, hidden)]


class Held:
    def __init__(self, ref):
        self.ref = ref

    def begin(self):
        pass

    def __call__(self):
        return self.ref


class Late:
    def __init__(self, copies, source, target):
        self.copies, self.source, self.target, self.ready = copies, source, target, None

    def begin(self):
        if self.ready is None:
            self.ready = self.copies.later(self.source, self.target)

    def __call__(self):
        self.begin()
        return self.ready()


class Copies:
    def __init__(self, sems):
        self.sems, self.open = sems, []

    def start(self, source, target):
        copy = pltpu.make_async_copy(source, target, self.sems.at[len(self.open)])
        copy.start()
        self.open.append(copy)

    def wait(self, index):
        if self.open[index] is not None:
            self.open[index].wait()
            self.open[index] = None

    def later(self, source, target):
        index = len(self.open)
        self.start(source, target)

        def ready():
            self.wait(index)
            return target

        return ready

    def finish(self):
        for index in range(len(self.open)):
            self.wait(index)


def first_kernel(scatter, x_hbm, *refs):
    sources, outs, refs = refs[:4], refs[4:8], refs[8:]
    x_next, held, held_next, x, sems = refs[0], refs[1:5], refs[5:9], refs[9], refs[10]
    copies = Copies(sems)
    tokens = [
        copies.later(x_hbm.at[pl.ds(0, 8), pl.ds(w * 8, 8)], x.at[w]) for w in range(4)
    ]
    weights = [Late(copies, s.at[0], d) for s, d in zip(sources, held)]
    weights[0].begin()
    ahead = [Late(copies, x_hbm.at[pl.ds(8, 8), pl.ds(w * 8, 8)], x_next.at[w]) for w in range(4)]
    ahead += [Late(copies, s.at[1], d) for s, d in zip(sources, held_next)]
    streams = ordered([lambda t=t: t()[...] for t in tokens])
    put_plain(block(streams, weights, PLAIN, [(None, None)] * 4, ahead), scatter, outs)
    copies.finish()


def second_kernel(scatter, x, side, wqkv, wproj, wup, wdown, *outs):
    outs[0][0:1] = side[...]
    weights = [Held(w) for w in (wqkv, wproj, wup, wdown)]
    streams = ordered([lambda w=w: x[w] for w in range(4)])
    put_plain(block(streams, weights, PLAIN, [(None, None)] * 4), scatter, outs)


def ordered(windows):
    row = lax.broadcasted_iota(jnp.int32, (256, 256), 0)
    col = lax.broadcasted_iota(jnp.int32, (256, 256), 1)
    quarter, level, inner, q = row // 64, row // 16 % 4, row // 4 % 4, row % 4
    r = quarter // 2 * 4 + inner // 2 * 2 + q % 2
    c = quarter % 2 * 4 + inner % 2 * 2 + q // 2
    order = jnp.where(col == (r * 8 + c) * 4 + level, 1.0, 0.0).astype(jnp.bfloat16)
    streams = []
    for window in windows:
        tokens = window().astype(jnp.float32)
        streams.append(dot(order, tokens.reshape(256, 512).astype(jnp.bfloat16)))
    return streams


def put_plain(streams, scatter, outs):
    for stream, pieces in zip(streams, scatter):
        done = stream.astype(jnp.bfloat16).reshape(4, 64, 512)
        for n, at, to, size in pieces:
            outs[n][to : to + size] = done[at : at + size]


def merge(streams, wmerge, scratch):
    for w, stream in enumerate(streams):
        for t in range(4):
            scratch[w, t] = stream[:, t * 128 : (t + 1) * 128]
    normed = []
    for w in range(len(streams)):
        pieces = [
            jnp.concatenate([scratch[w, t, pl.ds(q, 64, stride=4), :] for t in range(4)], axis=1)
            for q in range(4)
        ]
        normed.append(normalize(jnp.concatenate(pieces, axis=1)).astype(jnp.bfloat16))
    merged = dot(jnp.concatenate(normed, axis=0), wmerge[...]).astype(jnp.bfloat16)
    row = lax.broadcasted_iota(jnp.int32, (64, 64), 0)
    col = lax.broadcasted_iota(jnp.int32, (64, 64), 1)
    r, c, level = row // 16, row // 4 % 4, row % 4
    at = ((r // 2 * 2 + c // 2) * 4 + level) * 4 + r % 2 * 2 + c % 2
    order = jnp.where(col == at, 1.0, 0.0).astype(jnp.bfloat16)
    return [dot(order, merged[w * 64 : (w + 1) * 64]) for w in range(len(streams))]


def shifted_windows(count, edges, gather, ins, weights, wmerge, scratch):
    plain = group_biases(None)
    if edges:
        cut = lax.axis_index("lat") == lax.axis_size("lat") - 1
        split = group_biases(cut)
    biases = [split if w < edges else plain for w in range(count)]
    streams = []
    for w in range(count):
        pieces = [ins[n][at : at + size] for n, at, size in gather[w]]
        streams.append(jnp.concatenate(pieces, axis=0).reshape(256, 512).astype(jnp.float32))
    weights = [Held(w) for w in weights]
    streams = block(streams, weights, SHIFTED, biases)
    rows = merge(streams, wmerge, scratch)
    return [r.reshape(4, 4, 4, 1024).astype(jnp.bfloat16) for r in rows]


def third_kernel(gather, scatter, n_in, n_out, *refs):
    ins, refs = refs[:n_in], refs[n_in:]
    *weights, wmerge = refs[:5]
    outs, scratch = refs[5 : 5 + n_out], refs[5 + n_out]
    rows = shifted_windows(len(gather), 4, gather, ins, weights, wmerge, scratch)
    for w, done in enumerate(rows):
        for n, r, c, to_r, to_c, size_r, size_c in scatter[w]:
            outs[n][to_r : to_r + size_r, to_c : to_c + size_c] = done[r : r + size_r, c : c + size_c]


def fourth_kernel(gather, n_in, edge, side, *refs):
    ins, refs = refs[:n_in], refs[n_in:]
    *weights, wmerge, out, scratch, done, sems = refs
    copies = Copies(sems)
    copies.start(edge, out.at[pl.ds(6, 2), pl.ds(2, 14)])
    copies.start(side, out.at[pl.ds(2, 4), pl.ds(14, 2)])
    rows = shifted_windows(len(gather), 0, gather, ins, weights, wmerge, scratch)
    for w, row in enumerate(rows):
        done[w] = row
        copies.start(done.at[w], out.at[pl.ds(2, 4), pl.ds(2 + 4 * w, 4)])
    copies.finish()


def finish_kernel(lat, diag, lon, partial, out, sems):
    copies = Copies(sems)
    copies.start(lat, out.at[pl.ds(0, 2), pl.ds(2, 14)])
    copies.start(diag, out.at[pl.ds(0, 2), pl.ds(0, 2)])
    copies.start(lon, out.at[pl.ds(2, 6), pl.ds(0, 2)])
    copies.finish()


ANY = pl.BlockSpec(memory_space=pl.ANY)
VMEM = pl.BlockSpec(memory_space=pltpu.VMEM)
HBM = pl.BlockSpec(memory_space=pltpu.HBM)


def quarters(count):
    return jax.ShapeDtypeStruct((count, 64, 512), jnp.bfloat16)


def merged_shape(rows, cols):
    return jax.ShapeDtypeStruct((rows, cols, 4, 1024), jnp.bfloat16)


def cost(windows, merging):
    flops = windows * (2 * 256 * (512 * 6144) + 4 * 8 * 256 * 128 * 64)
    flops += windows * merging * 2 * 64 * 2048 * 1024
    return pl.CostEstimate(flops=flops, bytes_accessed=8 << 20, transcendentals=windows * 256 * 3072)


def shift(values, lat, lon, back):
    rows, cols = lax.axis_size("lat"), lax.axis_size("lon")
    pairs = []
    for i in range(rows):
        for j in range(cols):
            near, far = i * cols + j, (i + lat) % rows * cols + (j + lon) % cols
            pairs.append((far, near) if back else (near, far))
    return lax.ppermute(values, ("lat", "lon"), pairs)


def merge_scratch(count):
    return pltpu.VMEM((count, 4, 256, 128), jnp.float32)


def params(limit):
    return pltpu.CompilerParams(vmem_limit_bytes=limit << 20)


def body(patches, qkv_weight, proj_weight, up_weight, down_weight, merge_weight):
    sources = (qkv_weight, proj_weight, up_weight, down_weight)
    held = [jax.ShapeDtypeStruct(shape, jnp.bfloat16) for shape in WEIGHTS]
    scatter = [((3, 0, 0, 1), (0, 1, 0, 1), (2, 2, 0, 1), (1, 3, 0, 1))]
    scatter += [((0, 0, 2 * c - 1, 2), (1, 2, 2 * c - 1, 2)) for c in range(1, 4)]
    up, row1, side, corner, x_next, *held = pl.pallas_call(
        functools.partial(first_kernel, scatter),
        in_specs=[HBM] * 5,
        out_specs=[VMEM] * 13,
        out_shape=[
            quarters(7),
            quarters(7),
            quarters(1),
            quarters(1),
            jax.ShapeDtypeStruct((4, 8, 8, 4, 512), jnp.bfloat16),
            *held,
            *held,
        ],
        scratch_shapes=[
            pltpu.VMEM((4, 8, 8, 4, 512), jnp.bfloat16),
            pltpu.SemaphoreType.DMA((16,)),
        ],
        compiler_params=params(LIMITS[0]),
        cost_estimate=cost(4, 0),
        name="plain_upper",
    )(patches, *sources)
    up = shift(up, 1, 0, True)
    corner = shift(corner, 1, 1, True)
    scatter = [((0, 0, 1, 1), (1, 1, 0, 1), (0, 2, 2, 1), (2, 3, 0, 1))]
    scatter += [((1, 0, 2 * c - 1, 2), (2, 2, 2 * c - 1, 2)) for c in range(1, 4)]
    left, row2, row3 = pl.pallas_call(
        functools.partial(second_kernel, scatter),
        in_specs=[VMEM] * 6,
        out_specs=[VMEM] * 3,
        out_shape=[quarters(3), quarters(7), quarters(7)],
        compiler_params=params(LIMITS[1]),
        cost_estimate=cost(4, 0),
        name="plain_lower",
    )(x_next, side, *held[:4])
    weights_next = held[4:]
    left = shift(left, 0, 1, True)
    gather = [((2, 2 * w, 2), (3, 2 * w, 2)) for w in range(3)]
    gather.append(((2, 6, 1), (4, 2, 1), (3, 6, 1), (5, 0, 1)))
    gather.append(((0, 6, 1), (4, 0, 1), (1, 6, 1), (4, 1, 1)))
    scatter = [((0, 0, 0, 0, 4 * w, 2, 4), (1, 2, 0, 0, 4 * w, 2, 4)) for w in range(3)]
    scatter.append(
        ((0, 0, 0, 0, 12, 2, 2), (3, 0, 2, 4, 0, 2, 2), (1, 2, 0, 0, 12, 2, 2), (2, 2, 2, 0, 0, 2, 2))
    )
    scatter.append(((4, 0, 0, 0, 0, 4, 2), (3, 0, 2, 0, 0, 4, 2)))
    edge, lat, diag, lon, side = pl.pallas_call(
        functools.partial(third_kernel, gather, scatter, 6, 5),
        in_specs=[VMEM] * 11,
        out_specs=[VMEM] * 5,
        out_shape=[
            merged_shape(2, 14),
            merged_shape(2, 14),
            merged_shape(2, 2),
            merged_shape(6, 2),
            merged_shape(4, 2),
        ],
        scratch_shapes=[merge_scratch(5)],
        compiler_params=params(LIMITS[2]),
        cost_estimate=cost(5, 1),
        name="shifted_sent",
    )(row1, row2, row3, up, left, corner, *weights_next, merge_weight)
    lat = shift(lat, 1, 0, False)
    diag = shift(diag, 1, 1, False)
    lon = shift(lon, 0, 1, False)
    gather = [((0, 2 * w, 2), (1, 2 * w, 2)) for w in range(3)]
    out = pl.pallas_call(
        functools.partial(fourth_kernel, gather, 2),
        in_specs=[VMEM] * 9,
        out_specs=HBM,
        out_shape=merged_shape(8, 16),
        scratch_shapes=[
            merge_scratch(3),
            pltpu.VMEM((3, 4, 4, 4, 1024), jnp.bfloat16),
            pltpu.SemaphoreType.DMA((5,)),
        ],
        compiler_params=params(LIMITS[3]),
        cost_estimate=cost(3, 1),
        name="shifted_kept",
    )(edge, side, row1, row2, *weights_next, merge_weight)
    return pl.pallas_call(
        finish_kernel,
        in_specs=[VMEM] * 3 + [HBM],
        out_specs=HBM,
        out_shape=merged_shape(8, 16),
        input_output_aliases={3: 0},
        scratch_shapes=[pltpu.SemaphoreType.DMA((3,))],
        compiler_params=params(LIMITS[4]),
        name="finish",
    )(lat, diag, lon, out)


def solution(mesh):
    return jax.shard_map(
        body,
        mesh=mesh,
        in_specs=(P("lat", "lon", None, None), P(), P(), P(), P(), P()),
        out_specs=P("lat", "lon", None, None),
        check_vma=False,
    )
```
